128 devices in a mesh: space: 32 (over x, z, core), col: 4 (over y).
Axes of the slice: x: 4, y: 4, z: 4, core: 2. Of those that a mesh axis runs over, the one named last changes fastest.
Arguments:
- test_matrix: bfloat16 [256, 3712], P('col'), may hold values from -6 to 6
- anomalies: bfloat16 [3712, 65536], P(None, 'space'), may hold values from -32 to 32
Outputs:
- eofs: float32 [256, 65536], P('col', 'space')
- pcs: float32 [256, 3712], P('col')
The draws below stay inside these ranges and needn't reach their ends.
All inputs are finite; a program needn't handle non-finite values.
Results may differ from the reference program's by a relative error of at most 0.03.
Values may be sent and summed in bfloat16 or wider, within the bound.
A program may use at most 64 MiB of HBM per device.

```python
import jax
import jax.numpy as jnp
from jax import lax

BLOCK = 256
DAYS = 3712
ITERS = 2
POINTS = 65536


def draw_anomalies(key, part):
    key = jax.random.fold_in(key, 7)
    noise_key, time_key, row_key = jax.random.split(key, 3)
    position = jnp.arange(POINTS, dtype=jnp.float32) / POINTS
    row_scale = jnp.exp(jax.random.uniform(row_key, (POINTS,), jnp.float32, jnp.log(0.3), jnp.log(3.0)))
    row_scale = row_scale * jnp.exp(jnp.log(3.0) * (position - 0.5))
    time_scale = jnp.exp(jax.random.uniform(time_key, (DAYS,), jnp.float32, jnp.log(0.5), jnp.log(1.5)))
    noise = jax.random.truncated_normal(noise_key, -4.0, 4.0, (DAYS, POINTS), jnp.float32)
    return (noise * time_scale[:, None] * row_scale[None, :]).astype(jnp.bfloat16)


def steps_of(stream_key, extent, cuts, smallest, top_value):
    factor_of = 1.0
    for dim, blocks in cuts:
        heights = jax.random.uniform(jax.random.fold_in(jax.random.fold_in(stream_key, 6), dim), (blocks,), jnp.float32, smallest / len(cuts), top_value / len(cuts))
        factor_of = factor_of * jnp.repeat(jnp.exp(heights), extent[dim] // blocks).reshape((-1,) + (1,) * (len(extent) - 1 - dim))
    return factor_of


def normal_values(own_key, shape, scale, bound, shards=(), kind=jnp.bfloat16):
    drawn = jax.random.normal(own_key, shape, jnp.float32) * scale
    if len(shards) > 0:
        drawn = steps_of(own_key, shape, shards, -0.22, 0.18) * drawn
    return jnp.clip(drawn, min=-bound, max=bound).astype(kind)


def setup_inputs(seed: int = 0) -> dict:
    keys = jax.random.split(jax.random.key(seed), 3)
    test_matrix = normal_values(keys[0], (BLOCK, DAYS), 1.0, 6.0, ((0, 4),))
    anomalies = draw_anomalies(jax.random.fold_in(keys[2], 71), 0)
    return dict(test_matrix=test_matrix, anomalies=anomalies)


def contract_rows(first, second):
    return lax.dot_general(first.astype(jnp.float32), second.astype(jnp.float32), (((1,), (1,)), ((), ())), preferred_element_type=jnp.float32)

def reference(test_matrix, anomalies):
    left_factor = test_matrix
    orthonormal = None
    projected = None
    for iteration in range(ITERS + 1):
        basis_rows = jnp.dot(left_factor.astype(jnp.float32), anomalies.astype(jnp.float32), preferred_element_type=jnp.float32).astype(jnp.bfloat16)
        gram_sum = contract_rows(basis_rows, basis_rows) / POINTS
        lower_factor = jnp.linalg.cholesky(gram_sum)
        identity_matrix = jnp.eye(gram_sum.shape[0], dtype=jnp.float32)
        inverse = jax.scipy.linalg.solve_triangular(lower_factor, identity_matrix, lower=True).astype(jnp.bfloat16)
        orthonormal = jnp.dot(inverse.astype(jnp.float32), basis_rows.astype(jnp.float32), preferred_element_type=jnp.float32)
        projected = contract_rows(orthonormal.astype(jnp.bfloat16), anomalies) / POINTS
        left_factor = projected.astype(jnp.bfloat16)
    return (orthonormal, projected)
```

```python
import jax
import jax.numpy as jnp
from jax import lax
from jax.experimental import pallas as pl
from jax.experimental.pallas import tpu as pltpu
from jax.sharding import PartitionSpec as P

f32, bf16 = jnp.float32, jnp.bfloat16
MESH = pl.DeviceIdType.MESH
PASSES = 3
ROWS, DAYS, POINTS = 256, 3712, 65536
LOCAL = 2048
OWN = 512
GROUP = 1280
PADDED = 3 * GROUP
PANEL = 32
CHUNKS = [(i * 512, 512) for i in range(7)] + [(3584, 128)]


def split3(a):
    first = a.astype(bf16)
    rest = a - first.astype(f32)
    second = rest.astype(bf16)
    return first, second, (rest - second.astype(f32)).astype(bf16)


def dot_split(a, b):
    a0, a1, a2 = split3(a)
    b0, b1, b2 = split3(b)
    left = jnp.concatenate([a0, a0, a1, a1, a0, a2], axis=1)
    right = jnp.concatenate([b0, b1, b0, b1, b2, b0], axis=0)
    return jnp.dot(left, right, preferred_element_type=f32)


def invert_panel(block):
    b = block.shape[0]
    tiles = b // 8
    sub = lax.broadcasted_iota(jnp.int32, (8, 128), 0)
    lane = lax.broadcasted_iota(jnp.int32, (8, 128), 1)
    cols = [
        [
            jnp.broadcast_to(block[8 * t : 8 * t + 8, c : c + 1], (8, 128)) if t >= c // 8 else None
            for t in range(tiles)
        ]
        for c in range(b)
    ]
    pivots = [None] * tiles

    def spread(v, i):
        return jnp.broadcast_to(v[i : i + 1, :], (8, 128))

    for j in range(b):
        tj, ij = j // 8, j % 8
        pivot = spread(cols[j][tj], ij)
        scale = 1.0 / pivot
        pivots[tj] = pivot if pivots[tj] is None else jnp.where(sub == ij, pivot, pivots[tj])
        col = cols[j]
        mult = [None] * tiles
        for t in range(tj, tiles):
            v = col[t] * scale
            mult[t] = jnp.where(sub > ij, v, 0.0) if t == tj else v
        for c in range(j + 1, b):
            a = spread(col[c // 8], c % 8)
            for t in range(c // 8, tiles):
                cols[c][t] = cols[c][t] - mult[t] * a
        for c in range(j):
            a = spread(cols[c][tj], ij)
            for t in range(tj, tiles):
                cols[c][t] = cols[c][t] - mult[t] * a
        cols[j] = [None] * tj + [
            (jnp.where(sub == ij, 1.0, -mult[t]) if t == tj else -mult[t]) for t in range(tj, tiles)
        ]
    out = []
    for t in range(tiles):
        acc = jnp.zeros((8, 128), f32)
        for c in range(8 * t + 8):
            acc = jnp.where(lane == c, cols[c][t], acc)
        acc = acc * lax.rsqrt(pivots[t])
        out.append(jnp.where(lane <= sub + 8 * t, acc, 0.0))
    return jnp.concatenate(out, axis=0)[:, :b]


def factor_step(t_ref, step):
    s, e = step * PANEL, (step + 1) * PANEL
    inv = invert_panel(t_ref[s:e, s:e])
    col = lax.broadcasted_iota(jnp.int32, (PANEL, ROWS), 1)
    row = lax.broadcasted_iota(jnp.int32, (PANEL, ROWS), 0)
    own = jnp.where((col >= s) & (col < e), jnp.where(col - s == row, 1.0, 0.0), t_ref[s:e, :])
    new = dot_split(inv, own)
    if e < ROWS:
        below = dot_split(t_ref[e:, s:e], inv.T)
        t_ref[e:, s:e] = jnp.zeros((ROWS - e, PANEL), f32)
        t_ref[e:, :] -= dot_split(below, new)
    t_ref[s:e, :] = jnp.where(col < e, new, 0.0)


def kernel(
    test_ref, a_hbm, eofs_ref, pcs_ref,
    a_ref, yacc, yown, basis, full, left, inv_ref, t_ref,
    wp, wc, ws, wf, r1, s2, r2, x3,
    gp, gc, g1, g2, g3, gf,
    a_sem, y_ss, y_rs, wc_ss, wc_rs, w_ss, w_rs, gc_ss, gc_rs, g_ss, g_rs,
):
    space, y = lax.axis_index("space"), lax.axis_index("col")
    at = (space // 8, y, (space // 2) % 4)
    core = space % 2

    def peer(axis, d):
        x, yy, z = (((at[i] + d) % 4) if i == axis else at[i] for i in range(3))
        return ((x * 4 + z) * 2 + core, yy)

    sibling = (space + 1 - 2 * core, y)

    def send(src, dst, ss, rs, device):
        copy = pltpu.make_async_remote_copy(
            src_ref=src, dst_ref=dst, send_sem=ss, recv_sem=rs, device_id=device, device_id_type=MESH
        )
        copy.start()
        return copy

    loads = []
    for i, (s, n) in enumerate(CHUNKS):
        copy = pltpu.make_async_copy(a_hbm.at[s : s + n, :], a_ref.at[s : s + n, :], a_sem.at[i])
        copy.start()
        loads.append(copy)

    barrier = pltpu.get_barrier_semaphore()
    for axis in range(3):
        for d in (1, 2, 3):
            pl.semaphore_signal(barrier, inc=1, device_id=peer(axis, d), device_id_type=MESH)
    pl.semaphore_signal(barrier, inc=1, device_id=sibling, device_id_type=MESH)

    wp[:, DAYS:] = jnp.zeros((ROWS, PADDED - DAYS), bf16)
    for i, (s, n) in enumerate(CHUNKS):
        loads[i].wait()
        part = jnp.dot(test_ref[:, s : s + n], a_ref[s : s + n, :], preferred_element_type=f32)
        if i == 0:
            yacc[...] = part
        elif i < len(CHUNKS) - 1:
            yacc[...] += part
        else:
            yown[...] = (yacc[...] + part).astype(bf16)

    pl.semaphore_wait(barrier, 10)

    my_rows = pl.ds(pl.multiple_of(64 * y, 64), 64)
    copies = []
    for d in (1, 2, 3):
        there = pl.ds(pl.multiple_of(OWN * ((y + d) % 4), OWN), OWN)
        copies.append(send(yown.at[:, there], basis.at[my_rows, :], y_ss.at[d - 1], y_rs.at[d - 1], peer(1, d)))
    own_points = pl.ds(pl.multiple_of(OWN * y, OWN), OWN)
    basis[my_rows, :] = yown[:, own_points]
    for copy in copies:
        copy.wait()

    half = pl.ds(pl.multiple_of(128 * core, 128), 128)
    other = pl.ds(pl.multiple_of(128 * (1 - core), 128), 128)
    g_own = pl.multiple_of(192 * core, 64)
    g_other = pl.multiple_of(192 * (1 - core), 64)

    def order(g):
        return g, (g + 1) % 3, (g + 2) % 3

    def full_block(i):
        full[:, i * OWN : (i + 1) * OWN] = jnp.dot(
            left[...], a_ref[:, i * OWN : (i + 1) * OWN], preferred_element_type=f32
        ).astype(bf16)

    def one_pass(k, carry):
        sent = []
        last = k == PASSES - 1

        gram = lax.dot_general(basis[...], basis[...], (((1,), (1,)), ((), ())), preferred_element_type=f32)
        gp[:ROWS, :] = gram[:, :128]
        gp[ROWS:, :] = gram[128:, 128:]
        g_core = send(gp.at[pl.ds(g_other, 192), :], gc, gc_ss.at[0], gc_rs.at[0], sibling)
        sent.append(g_core)

        w_core = []
        for g in range(3):
            s = GROUP * g
            n = min(GROUP, DAYS - s)
            wp[:, s : s + n] = lax.dot_general(
                basis[...], a_ref[s : s + n, own_points], (((1,), (1,)), ((), ())), preferred_element_type=f32
            ).astype(bf16)
            w_core.append(
                send(wp.at[other, s : s + GROUP], wc.at[:, s : s + GROUP], wc_ss.at[0, g], wc_rs.at[0, g], sibling)
            )
        sent += w_core

        def gram_send(stage, buf, g, value):
            axis = order(g)[stage]
            me = at[axis]
            buf[g, me] = value
            out = [
                send(buf.at[g, me], buf.at[g, me], g_ss.at[stage, g, d - 1], g_rs.at[stage, g, d - 1], peer(axis, d))
                for d in (1, 2, 3)
            ]
            sent.extend(out)
            return out

        def gram_sum(copies, buf, g):
            for copy in copies:
                copy.wait_recv()
            return (buf[g, 0] + buf[g, 1]) + (buf[g, 2] + buf[g, 3])

        g_core.wait_recv()
        gs1 = [
            gram_send(0, g1, g, gp[pl.ds(g_own + 64 * g, 64), :] + gc[64 * g : 64 * g + 64, :]) for g in range(3)
        ]

        ws1 = []
        for g in range(3):
            w_core[g].wait_recv()
            s = GROUP * g
            ws[:, s : s + GROUP] = (wp[half, s : s + GROUP].astype(f32) + wc[:, s : s + GROUP].astype(f32)).astype(bf16)
            axis = order(g)[0]
            for d in (1, 2, 3):
                rows = pl.ds(pl.multiple_of(32 * ((at[axis] + d) % 4), 32), 32)
                ws1.append(
                    send(
                        ws.at[rows, s : s + GROUP], r1.at[g, d - 1], w_ss.at[0, g, d - 1], w_rs.at[0, g, d - 1],
                        peer(axis, d),
                    )
                )
        sent += ws1

        pl.when(last)(lambda: full_block(0))

        gs2 = [gram_send(1, g2, g, gram_sum(gs1[g], g1, g)) for g in range(3)]

        ws2 = []
        for g in range(3):
            for copy in ws1[3 * g : 3 * g + 3]:
                copy.wait_recv()
            s = GROUP * g
            axis = order(g)[0]
            rows = pl.ds(pl.multiple_of(32 * at[axis], 32), 32)
            total = ws[rows, s : s + GROUP].astype(f32)
            for d in range(3):
                total += r1[g, d].astype(f32)
            s2[g] = total.astype(bf16)
            axis = order(g)[1]
            for d in (1, 2, 3):
                q = (at[axis] + d) % 4
                piece = s2.at[
                    g, pl.ds(pl.multiple_of(16 * (q // 2), 16), 16), pl.ds(pl.multiple_of(640 * (q % 2), 128), 640)
                ]
                ws2.append(send(piece, r2.at[g, d - 1], w_ss.at[1, g, d - 1], w_rs.at[1, g, d - 1], peer(axis, d)))
        sent += ws2

        pl.when(last)(lambda: full_block(1))

        gs3 = [gram_send(2, g3, g, gram_sum(gs2[g], g2, g)) for g in range(3)]

        ws3 = []
        for g in range(3):
            for copy in ws2[3 * g : 3 * g + 3]:
                copy.wait_recv()
            q = at[order(g)[1]]
            total = s2[
                g, pl.ds(pl.multiple_of(16 * (q // 2), 16), 16), pl.ds(pl.multiple_of(640 * (q % 2), 128), 640)
            ].astype(f32)
            for d in range(3):
                total += r2[g, d].astype(f32)
            axis = order(g)[2]
            me = at[axis]
            x3[g, me] = total.astype(bf16)
            for d in (1, 2, 3):
                ws3.append(
                    send(
                        x3.at[g, me], x3.at[g, me], w_ss.at[2, g, d - 1], w_rs.at[2, g, d - 1], peer(axis, d)
                    )
                )
        sent += ws3

        pl.when(last)(lambda: full_block(2))

        for g in range(3):
            gf[pl.ds(g_own + 64 * g, 64), :] = gram_sum(gs3[g], g3, g)
        g_back = send(
            gf.at[pl.ds(g_own, 192), :], gf.at[pl.ds(g_own, 192), :], gc_ss.at[1], gc_rs.at[1], sibling
        )
        sent.append(g_back)

        def spread_piece(g, quarter):
            first, second, _ = order(g)
            row, day = 128 * core + 32 * at[first], GROUP * g
            if quarter:
                return wf.at[pl.ds(pl.multiple_of(row, 32), 32), day : day + GROUP]
            q = at[second]
            return wf.at[
                pl.ds(pl.multiple_of(row + 16 * (q // 2), 16), 16),
                pl.ds(pl.multiple_of(day + 640 * (q % 2), 128), 640),
            ]

        ws4 = []
        for g in range(3):
            for copy in ws3[3 * g : 3 * g + 3]:
                copy.wait_recv()
            parts = [x3[g, i].astype(f32) for i in range(4)]
            piece = spread_piece(g, False)
            piece[...] = ((parts[0] + parts[1]) + (parts[2] + parts[3])).astype(bf16)
            axis = order(g)[1]
            for d in (1, 2, 3):
                ws4.append(send(piece, piece, w_ss.at[3, g, d - 1], w_rs.at[3, g, d - 1], peer(axis, d)))
        sent += ws4

        pl.when(last)(lambda: full_block(3))

        g_back.wait_recv()
        scale = 1.0 / POINTS
        t_ref[:, :128] = gf[:ROWS, :] * scale
        t_ref[128:, 128:] = gf[ROWS:, :] * scale
        t_ref[:128, 128:] = gf[128:ROWS, :].T * scale

        steps = ROWS // PANEL
        for step in range(0, 2):
            factor_step(t_ref, step)

        ws5 = []
        for g in range(3):
            for copy in ws4[3 * g : 3 * g + 3]:
                copy.wait_recv()
            piece = spread_piece(g, True)
            axis = order(g)[0]
            for d in (1, 2, 3):
                ws5.append(send(piece, piece, w_ss.at[4, g, d - 1], w_rs.at[4, g, d - 1], peer(axis, d)))
        sent += ws5

        for step in range(2, 7):
            factor_step(t_ref, step)

        w_back = []
        for g in range(3):
            for copy in ws5[3 * g : 3 * g + 3]:
                copy.wait_recv()
            s = GROUP * g
            w_back.append(
                send(wf.at[half, s : s + GROUP], wf.at[half, s : s + GROUP], wc_ss.at[1, g], wc_rs.at[1, g], sibling)
            )
        sent += w_back

        for step in range(7, steps):
            factor_step(t_ref, step)
        inv_ref[...] = t_ref[...].astype(bf16)

        for copy in w_back:
            copy.wait_recv()

        @pl.when(jnp.logical_not(last))
        def _():
            left[...] = (jnp.dot(inv_ref[...], wf[:, :DAYS], preferred_element_type=f32) * scale).astype(bf16)
            basis[...] = jnp.dot(left[...], a_ref[:, own_points], preferred_element_type=f32).astype(bf16)

        for copy in sent:
            copy.wait_send()
        return carry

    lax.fori_loop(0, PASSES, one_pass, 0)

    own_inverse = inv_ref[my_rows, :]
    eofs_ref[...] = jnp.dot(own_inverse, full[...], preferred_element_type=f32)
    pcs_ref[...] = jnp.dot(own_inverse, wf[:, :DAYS], preferred_element_type=f32) * (1.0 / POINTS)


def body(test_matrix, anomalies):
    vmem = pl.BlockSpec(memory_space=pltpu.VMEM)
    dma = pltpu.SemaphoreType.DMA
    return pl.pallas_call(
        kernel,
        out_shape=(jax.ShapeDtypeStruct((64, LOCAL), f32), jax.ShapeDtypeStruct((64, DAYS), f32)),
        in_specs=[vmem, pl.BlockSpec(memory_space=pl.ANY)],
        out_specs=(vmem, vmem),
        scratch_shapes=[
            pltpu.VMEM((DAYS, LOCAL), bf16),
            pltpu.VMEM((64, LOCAL), f32),
            pltpu.VMEM((64, LOCAL), bf16),
            pltpu.VMEM((ROWS, OWN), bf16),
            pltpu.VMEM((ROWS, LOCAL), bf16),
            pltpu.VMEM((ROWS, DAYS), bf16),
            pltpu.VMEM((ROWS, ROWS), bf16),
            pltpu.VMEM((ROWS, ROWS), f32),
            pltpu.VMEM((ROWS, PADDED), bf16),
            pltpu.VMEM((128, PADDED), bf16),
            pltpu.VMEM((128, PADDED), bf16),
            pltpu.VMEM((ROWS, PADDED), bf16),
            pltpu.VMEM((3, 3, 32, GROUP), bf16),
            pltpu.VMEM((3, 32, GROUP), bf16),
            pltpu.VMEM((3, 3, 16, 640), bf16),
            pltpu.VMEM((3, 4, 16, 640), bf16),
            pltpu.VMEM((384, 128), f32),
            pltpu.VMEM((192, 128), f32),
            pltpu.VMEM((3, 4, 64, 128), f32),
            pltpu.VMEM((3, 4, 64, 128), f32),
            pltpu.VMEM((3, 4, 64, 128), f32),
            pltpu.VMEM((384, 128), f32),
            dma((len(CHUNKS),)),
            dma((3,)),
            dma((3,)),
            dma((2, 3)),
            dma((2, 3)),
            dma((5, 3, 3)),
            dma((5, 3, 3)),
            dma((2,)),
            dma((2,)),
            dma((3, 3, 3)),
            dma((3, 3, 3)),
        ],
        compiler_params=pltpu.CompilerParams(collective_id=0, has_side_effects=True, vmem_limit_bytes=52 << 20),
        cost_estimate=pl.CostEstimate(flops=20 * 10**9, bytes_accessed=16 * 10**6, transcendentals=0),
        name="subspace_iteration",
    )(test_matrix, anomalies)


def solution(mesh):
    return jax.shard_map(
        body,
        mesh=mesh,
        in_specs=(P("col", None), P(None, "space")),
        out_specs=(P("col", "space"), P("col", None)),
        check_vma=False,
    )
```

```python
import jax
import jax.numpy as jnp
from jax import lax
from jax.experimental import pallas as pl
from jax.experimental.pallas import tpu as pltpu
from jax.sharding import PartitionSpec as P

f32, bf16 = jnp.float32, jnp.bfloat16
MESH = pl.DeviceIdType.MESH
PASSES = 3
ROWS, DAYS, POINTS = 256, 3712, 65536
LOCAL = 2048
OWN = 512
WIDTHS = [384] * 5 + [256] * 7
UNITS, WIDEST = len(WIDTHS), max(WIDTHS)
STARTS = [sum(WIDTHS[:u]) for u in range(UNITS + 1)]
BATCHES = (0, 6, UNITS)
PANEL, STRIP = 32, 16
FAR_FIRST = (2, 1, 3)
SCHEDULE = (("factor", 4), ("share", 0), ("share", 1), ("factor", 2), ("use", 0), ("factor", 1), ("use", 1), ("factor", 1))


def split3(a):
    first = a.astype(bf16)
    rest = a - first.astype(f32)
    second = rest.astype(bf16)
    return first, second, (rest - second.astype(f32)).astype(bf16)


def eliminate_panel(tiles, s):
    count = len(tiles)
    sub = lax.broadcasted_iota(jnp.int32, (8, 128), 0)
    sub_all = lax.broadcasted_iota(jnp.int32, (8, ROWS), 0)
    lane_all = lax.broadcasted_iota(jnp.int32, (8, ROWS), 1)
    rows = list(tiles)
    square, shift = [None] * count, [None] * count

    def spread(v, i):
        return jnp.broadcast_to(v[i : i + 1, :], v.shape)

    def wide(v):
        return jnp.concatenate([v, v], axis=1)

    for c0 in range(0, 8 * count, STRIP):
        q0, q1 = c0 // 8, (c0 + STRIP) // 8
        cols = [
            {
                t: jnp.broadcast_to(rows[t][:, s + c0 + c : s + c0 + c + 1], (8, 128))
                for t in range(q0 + c // 8, count)
            }
            for c in range(STRIP)
        ]
        inside = (lane_all >= s + c0) & (lane_all < s + c0 + STRIP)
        for t in range(count):
            unit = jnp.where(lane_all - s - 8 * t == sub_all, 1.0, 0.0) if q0 <= t < q1 else 0.0
            rows[t] = jnp.where(inside, unit, rows[t])
        for j in range(0, STRIP, 2):
            q, i = q0 + j // 8, j % 8
            x, y = cols[j], cols[j + 1]
            a, b, c = spread(x[q], i), spread(x[q], i + 1), spread(y[q], i + 1)
            over_a = 1.0 / a
            over_det = 1.0 / (a * c - b * b)
            an, bn, cn = a * over_det, b * over_det, c * over_det
            sq = jnp.where(sub == i, over_a, an)
            sh = jnp.where(sub == i + 1, -b * over_a, 0.0)
            square[q] = sq if i == 0 else jnp.where(sub >= i, sq, square[q])
            shift[q] = sh if i == 0 else jnp.where(sub >= i, sh, shift[q])
            first, second = spread(rows[q], i), spread(rows[q], i + 1)
            for t in range(q, count):
                u = cn * x[t] - bn * y[t]
                v = an * y[t] - bn * x[t]
                if t == q:
                    u = jnp.where(sub > i + 1, u, 0.0)
                    v = jnp.where(sub > i + 1, v, 0.0)
                for k in range(j + 2, STRIP):
                    tk = q0 + k // 8
                    if t >= tk:
                        cols[k][t] = cols[k][t] - u * spread(x[tk], k % 8) - v * spread(y[tk], k % 8)
                if t > q or i < 6:
                    rows[t] = rows[t] - wide(u) * first - wide(v) * second
    out = []
    for t in range(count):
        down = jnp.concatenate([rows[t][7:8], rows[t][0:7]], axis=0)
        out.append((rows[t] + wide(shift[t]) * down) * wide(jnp.sqrt(square[t])))
    return jnp.concatenate(out, axis=0)


def factor_step(t_ref, step):
    s, e = step * PANEL, (step + 1) * PANEL
    new = eliminate_panel([t_ref[s + 8 * t : s + 8 * t + 8, :] for t in range(PANEL // 8)], s)
    if e < ROWS:
        n0, n1, n2 = split3(new)
        left = jnp.concatenate([n0, n0, n1, n1, n0, n2], axis=0)
        right = jnp.concatenate([n0, n1, n0, n1, n2, n0], axis=0)
        skip = e // 128 * 128
        update = lax.dot_general(left[:, skip:], right, (((0,), (0,)), ((), ())), preferred_element_type=f32)
        col = lax.broadcasted_iota(jnp.int32, (ROWS - e, ROWS), 1)
        t_ref[e:, :] = jnp.where((col >= s) & (col < e), 0.0, t_ref[e:, :]) - update[e - skip :]
    col = lax.broadcasted_iota(jnp.int32, (PANEL, ROWS), 1)
    t_ref[s:e, :] = jnp.where(col < e, new, 0.0)


def kernel(
    test_hbm, a_hbm, eofs_ref, pcs_ref,
    test_ref, a_ref, yown, yacc, basis, full, inv_ref, t_ref, norm_ref,
    wp, wc, ws, wf, r1, x2, x3,
    gp, gc, g1, g2, g3, gf,
    test_sem, a_sem, y_ss, y_rs, wc_ss, wc_rs, w_ss, w_rs, gc_ss, gc_rs, g_ss, g_rs,
):
    space, y = lax.axis_index("space"), lax.axis_index("col")
    at = (space // 8, y, (space // 2) % 4)
    core = space % 2

    def peer(axis, d):
        x, yy, z = (((at[i] + d) % 4) if i == axis else at[i] for i in range(3))
        return ((x * 4 + z) * 2 + core, yy)

    sibling = (space + 1 - 2 * core, y)

    def copy_to(device, src, dst, ss, rs):
        return pltpu.make_async_remote_copy(
            src_ref=src, dst_ref=dst, send_sem=ss, recv_sem=rs, device_id=device, device_id_type=MESH
        )

    def send(device, src, dst, ss, rs):
        copy = copy_to(device, src, dst, ss, rs)
        copy.start()
        return copy

    def points(i):
        return pl.ds(pl.multiple_of(OWN * i, OWN), OWN)

    load_test = pltpu.make_async_copy(test_hbm, test_ref, test_sem.at[0])
    load_test.start()
    blocks = [(y + d) % 4 for d in FAR_FIRST] + [y]
    loads = []
    for i, block in enumerate(blocks):
        for h in range(2):
            part = (pl.ds(h * (DAYS // 2), DAYS // 2), points(block))
            copy = pltpu.make_async_copy(a_hbm.at[part], a_ref.at[part], a_sem.at[i, h])
            copy.start()
            loads.append(copy)

    barrier = pltpu.get_barrier_semaphore()
    for axis in range(3):
        for d in FAR_FIRST:
            pl.semaphore_signal(barrier, inc=1, device_id=peer(axis, d), device_id_type=MESH)
    pl.semaphore_signal(barrier, inc=1, device_id=sibling, device_id_type=MESH)

    load_test.wait()

    my_rows = pl.ds(pl.multiple_of(64 * y, 64), 64)
    first_copies = []
    for i, block in enumerate(blocks):
        loads[2 * i].wait()
        loads[2 * i + 1].wait()
        product = jnp.dot(test_ref[...], a_ref[:, points(block)], preferred_element_type=f32).astype(bf16)
        if i == 0:
            pl.semaphore_wait(barrier, 10)
        if i < 3:
            yown[i] = product
            first_copies.append(
                send(peer(1, FAR_FIRST[i]), yown.at[i], basis.at[my_rows, :], y_ss.at[i], y_rs.at[i])
            )
        else:
            basis[my_rows, :] = product
    for copy in first_copies:
        copy.wait()

    half = pl.ds(pl.multiple_of(128 * core, 128), 128)
    other = pl.ds(pl.multiple_of(128 * (1 - core), 128), 128)
    g_own = pl.multiple_of(192 * core, 64)
    g_other = pl.multiple_of(192 * (1 - core), 64)

    def order(g):
        return g % 3, (g + 1) % 3, (g + 2) % 3

    def days(u):
        return slice(STARTS[u], STARTS[u + 1])

    def rows_of(i):
        return pl.ds(pl.multiple_of(32 * i, 32), 32)

    def one_pass(k, carry):
        last = k == PASSES - 1
        now, before = k % 2, (k + 1) % 2
        def send_three(axis, pair, ss, rs, three):
            for d in FAR_FIRST:
                src, dst = pair(d)
                send(peer(axis, d), src, dst, ss, rs)
            return copy_to(sibling, three, three, ss, rs)

        def full_block(i):
            product = jnp.dot(
                wf[before], a_ref[:, i * OWN : (i + 1) * OWN], preferred_element_type=f32
            ).astype(bf16)
            full[:, i * OWN : (i + 1) * OWN] = (
                jnp.dot(inv_ref[...], product, preferred_element_type=f32) * (1.0 / POINTS)
            ).astype(bf16)

        gram = lax.dot_general(basis[...], basis[...], (((1,), (1,)), ((), ())), preferred_element_type=f32)
        gp[:ROWS, :] = gram[:, :128]
        gp[ROWS:, :] = gram[128:, 128:]
        g_core = send(sibling, gp.at[pl.ds(g_other, 192), :], gc, gc_ss.at[0], gc_rs.at[0])

        w_core = []
        for u in range(UNITS):
            wp[:, days(u)] = lax.dot_general(
                basis[...], a_ref[days(u), points(y)], (((1,), (1,)), ((), ())), preferred_element_type=f32
            ).astype(bf16)
            w_core.append(send(sibling, wp.at[other, days(u)], wc.at[:, days(u)], wc_ss.at[0], wc_rs.at[0, u]))

        def gram_send(stage, buf, g, value):
            axis = order(g)[stage]
            mine = buf.at[g, at[axis]]
            mine[...] = value
            return send_three(axis, lambda d: (mine, mine), g_ss.at[stage], g_rs.at[stage, g], buf.at[g, 0:3])

        def gram_sum(arrived, buf, g):
            arrived.wait_recv()
            return (buf[g, 0] + buf[g, 1]) + (buf[g, 2] + buf[g, 3])

        def four(buf, u):
            parts = [buf[u, i, :, : WIDTHS[u]].astype(f32) for i in range(4)]
            return ((parts[0] + parts[1]) + (parts[2] + parts[3])).astype(bf16)

        g_core.wait_recv()
        gs1 = [
            gram_send(0, g1, g, gp[pl.ds(g_own + 64 * g, 64), :] + gc[64 * g : 64 * g + 64, :]) for g in range(3)
        ]

        def slots(buf, u):
            return buf.at[u, 0:3, :, : WIDTHS[u]]

        ws1 = []
        for u in range(UNITS):
            w_core[u].wait_recv()
            ws[:, days(u)] = (wp[half, days(u)].astype(f32) + wc[:, days(u)].astype(f32)).astype(bf16)
            axis = order(u)[0]
            ws1.append(
                send_three(
                    axis,
                    lambda d, u=u, axis=axis: (
                        ws.at[rows_of((at[axis] + d) % 4), days(u)], r1.at[u, d - 1, :, : WIDTHS[u]]
                    ),
                    w_ss.at[0], w_rs.at[0, u], slots(r1, u),
                )
            )

        pl.when(last)(lambda: full_block(0))

        gs2 = [gram_send(1, g2, g, gram_sum(gs1[g], g1, g)) for g in range(3)]

        ws2 = []
        for u in range(UNITS):
            ws1[u].wait_recv()
            first, axis, _ = order(u)
            total = ws[rows_of(at[first]), days(u)].astype(f32)
            for d in range(3):
                total += r1[u, d, :, : WIDTHS[u]].astype(f32)
            mine = x2.at[u, at[axis], :, : WIDTHS[u]]
            mine[...] = total.astype(bf16)
            ws2.append(send_three(axis, lambda d, m=mine: (m, m), w_ss.at[1], w_rs.at[1, u], slots(x2, u)))

        pl.when(last)(lambda: full_block(1))

        gs3 = [gram_send(2, g3, g, gram_sum(gs2[g], g2, g)) for g in range(3)]

        ws3 = []
        for u in range(UNITS):
            ws2[u].wait_recv()
            axis = order(u)[2]
            mine = x3.at[u, at[axis], :, : WIDTHS[u]]
            mine[...] = four(x2, u)
            ws3.append(send_three(axis, lambda d, m=mine: (m, m), w_ss.at[2], w_rs.at[2, u], slots(x3, u)))

        pl.when(last)(lambda: full_block(2))

        ws4, pieces = [], []

        def finish(u):
            ws3[u].wait_recv()
            piece = wf.at[now, rows_of(4 * core + at[order(u)[0]]), days(u)]
            piece[...] = four(x3, u)
            pieces.append(piece)

        def send_back(u):
            ws4.append(
                send_three(
                    order(u)[0], lambda d: (pieces[u], pieces[u]), w_ss.at[3], w_rs.at[3, u], slots(x3, u)
                )
            )

        for u in range(UNITS - 3):
            finish(u)
            send_back(u)
        for g in range(3):
            gf[pl.ds(g_own + 64 * g, 64), :] = gram_sum(gs3[g], g3, g)
        g_mine = gf.at[pl.ds(g_own, 192), :]
        g_back = send(sibling, g_mine, g_mine, gc_ss.at[1], gc_rs.at[1])
        for u in range(UNITS - 3, UNITS):
            finish(u)
        for u in range(UNITS - 3, UNITS):
            send_back(u)

        pl.when(last)(lambda: full_block(3))

        stage = wp.at[0:96, :]
        for i in range(3):
            copy_to(sibling, stage, stage, w_ss.at[i], w_rs.at[i, 0]).wait_send()
            copy_to(sibling, g1.at[:, 0:3], g1.at[:, 0:3], g_ss.at[i], g_rs.at[i, 0]).wait_send()
        copy_to(sibling, wc, wc, wc_ss.at[0], wc_rs.at[0, 0]).wait_send()
        g_core.wait_send()

        g_back.wait_recv()
        t_ref[:, :128] = gf[:ROWS, :]
        t_ref[128:, 128:] = gf[ROWS:, :]
        t_ref[:128, 128:] = gf[128:ROWS, :].T
        gram = t_ref[...]
        diagonal = jnp.where(
            lax.broadcasted_iota(jnp.int32, (ROWS, ROWS), 0) == lax.broadcasted_iota(jnp.int32, (ROWS, ROWS), 1), gram, 0.0
        )
        across = lax.rsqrt(jnp.sum(diagonal, axis=0, keepdims=True))
        down = lax.rsqrt(jnp.sum(diagonal, axis=1, keepdims=True))
        t_ref[...] = gram * down * across
        norm_ref[...] = across * POINTS**0.5

        w_back = []
        step = 0
        for what, n in SCHEDULE:
            if what == "factor":
                for _ in range(n):
                    factor_step(t_ref, step)
                    step += 1
            elif what == "share":
                for u in range(BATCHES[n], BATCHES[n + 1]):
                    ws4[u].wait_recv()
                    mine = wf.at[now, half, days(u)]
                    w_back.append(send(sibling, mine, mine, wc_ss.at[1], wc_rs.at[1, u]))
            else:
                for u in range(BATCHES[n], BATCHES[n + 1]):
                    w_back[u].wait_recv()
                own = slice(STARTS[BATCHES[n]], STARTS[BATCHES[n + 1]])
                product = jnp.dot(wf[now, :, own], a_ref[own, points(y)], preferred_element_type=f32)
                yacc[...] = product if n == 0 else yacc[...] + product
        inverse = (t_ref[...] * norm_ref[...]).astype(bf16)
        inv_ref[...] = inverse
        basis[...] = (
            jnp.dot(inverse, yacc[...].astype(bf16), preferred_element_type=f32) * (1.0 / POINTS)
        ).astype(bf16)

        copy_to(sibling, stage, stage, w_ss.at[3], w_rs.at[3, 0]).wait_send()
        copy_to(sibling, wc, wc, wc_ss.at[1], wc_rs.at[1, 0]).wait_send()
        g_back.wait_send()
        return carry

    lax.fori_loop(0, PASSES, one_pass, 0)

    own_inverse = inv_ref[my_rows, :]
    eofs_ref[...] = jnp.dot(own_inverse, full[...], preferred_element_type=f32)
    pcs_ref[...] = jnp.dot(own_inverse, wf[(PASSES - 1) % 2, :, :], preferred_element_type=f32) * (1.0 / POINTS)


def body(test_matrix, anomalies):
    vmem = pl.BlockSpec(memory_space=pltpu.VMEM)
    hbm = pl.BlockSpec(memory_space=pl.ANY)
    dma = pltpu.SemaphoreType.DMA
    return pl.pallas_call(
        kernel,
        out_shape=(jax.ShapeDtypeStruct((64, LOCAL), f32), jax.ShapeDtypeStruct((64, DAYS), f32)),
        in_specs=[hbm, hbm],
        out_specs=(vmem, vmem),
        scratch_shapes=[
            pltpu.VMEM((64, DAYS), bf16),
            pltpu.VMEM((DAYS, LOCAL), bf16),
            pltpu.VMEM((3, 64, OWN), bf16),
            pltpu.VMEM((ROWS, OWN), f32),
            pltpu.VMEM((ROWS, OWN), bf16),
            pltpu.VMEM((ROWS, LOCAL), bf16),
            pltpu.VMEM((ROWS, ROWS), bf16),
            pltpu.VMEM((ROWS, ROWS), f32),
            pltpu.VMEM((1, ROWS), f32),
            pltpu.VMEM((ROWS, DAYS), bf16),
            pltpu.VMEM((128, DAYS), bf16),
            pltpu.VMEM((128, DAYS), bf16),
            pltpu.VMEM((2, ROWS, DAYS), bf16),
            pltpu.VMEM((UNITS, 3, 32, WIDEST), bf16),
            pltpu.VMEM((UNITS, 4, 32, WIDEST), bf16),
            pltpu.VMEM((UNITS, 4, 32, WIDEST), bf16),
            pltpu.VMEM((384, 128), f32),
            pltpu.VMEM((192, 128), f32),
            pltpu.VMEM((3, 4, 64, 128), f32),
            pltpu.VMEM((3, 4, 64, 128), f32),
            pltpu.VMEM((3, 4, 64, 128), f32),
            pltpu.VMEM((384, 128), f32),
            dma((1,)),
            dma((4, 2)),
            dma((3,)),
            dma((3,)),
            dma((2,)),
            dma((2, UNITS)),
            dma((4,)),
            dma((4, UNITS)),
            dma((2,)),
            dma((2,)),
            dma((3,)),
            dma((3, 3)),
        ],
        compiler_params=pltpu.CompilerParams(collective_id=0, has_side_effects=True, vmem_limit_bytes=52 << 20),
        cost_estimate=pl.CostEstimate(flops=20 * 10**9, bytes_accessed=16 * 10**6, transcendentals=0),
        name="subspace_iteration",
    )(test_matrix, anomalies)


def solution(mesh):
    return jax.shard_map(
        body,
        mesh=mesh,
        in_specs=(P("col", None), P(None, "space")),
        out_specs=(P("col", "space"), P("col", None)),
        check_vma=False,
    )
```

```python
import jax
import jax.numpy as jnp
from jax import lax
from jax.experimental import pallas as pl
from jax.experimental.pallas import tpu as pltpu
from jax.sharding import PartitionSpec as P

f32, bf16 = jnp.float32, jnp.bfloat16
MESH = pl.DeviceIdType.MESH
PASSES = 3
ROWS, DAYS, POINTS = 256, 3712, 65536
LOCAL = 2048
OWN = 512
WIDTHS = [384] * 5 + [256] * 7
UNITS, WIDEST = len(WIDTHS), max(WIDTHS)
STARTS = [sum(WIDTHS[:u]) for u in range(UNITS + 1)]
BATCHES = (0, 6, 10, UNITS)
AHEAD = 6
PANEL, STRIP = 32, 16
FAR_FIRST = (2, 1, 3)
SCHEDULE = (("factor", 4), ("share", 0), ("share", 1), ("share", 2), ("factor", 2), ("use", 0), ("factor", 1), ("use", 1), ("use", 2), ("factor", 1))


def split3(a):
    first = a.astype(bf16)
    rest = a - first.astype(f32)
    second = rest.astype(bf16)
    return first, second, (rest - second.astype(f32)).astype(bf16)


def eliminate_panel(tiles, s):
    count = len(tiles)
    sub = lax.broadcasted_iota(jnp.int32, (8, 128), 0)
    sub_all = lax.broadcasted_iota(jnp.int32, (8, ROWS), 0)
    lane_all = lax.broadcasted_iota(jnp.int32, (8, ROWS), 1)
    rows = list(tiles)
    square, shift = [None] * count, [None] * count

    def spread(v, i):
        return jnp.broadcast_to(v[i : i + 1, :], v.shape)

    def wide(v):
        return jnp.concatenate([v, v], axis=1)

    for c0 in range(0, 8 * count, STRIP):
        q0, q1 = c0 // 8, (c0 + STRIP) // 8
        cols = [
            {
                t: jnp.broadcast_to(rows[t][:, s + c0 + c : s + c0 + c + 1], (8, 128))
                for t in range(q0 + c // 8, count)
            }
            for c in range(STRIP)
        ]
        inside = (lane_all >= s + c0) & (lane_all < s + c0 + STRIP)
        for t in range(count):
            unit = jnp.where(lane_all - s - 8 * t == sub_all, 1.0, 0.0) if q0 <= t < q1 else 0.0
            rows[t] = jnp.where(inside, unit, rows[t])
        for j in range(0, STRIP, 2):
            q, i = q0 + j // 8, j % 8
            x, y = cols[j], cols[j + 1]
            a, b, c = spread(x[q], i), spread(x[q], i + 1), spread(y[q], i + 1)
            over_a = 1.0 / a
            over_det = 1.0 / (a * c - b * b)
            an, bn, cn = a * over_det, b * over_det, c * over_det
            sq = jnp.where(sub == i, over_a, an)
            sh = jnp.where(sub == i + 1, -b * over_a, 0.0)
            square[q] = sq if i == 0 else jnp.where(sub >= i, sq, square[q])
            shift[q] = sh if i == 0 else jnp.where(sub >= i, sh, shift[q])
            first, second = spread(rows[q], i), spread(rows[q], i + 1)
            for t in range(q, count):
                u = cn * x[t] - bn * y[t]
                v = an * y[t] - bn * x[t]
                if t == q:
                    u = jnp.where(sub > i + 1, u, 0.0)
                    v = jnp.where(sub > i + 1, v, 0.0)
                for k in range(j + 2, STRIP):
                    tk = q0 + k // 8
                    if t >= tk:
                        cols[k][t] = cols[k][t] - u * spread(x[tk], k % 8) - v * spread(y[tk], k % 8)
                if t > q or i < 6:
                    rows[t] = rows[t] - wide(u) * first - wide(v) * second
    out = []
    for t in range(count):
        down = jnp.concatenate([rows[t][7:8], rows[t][0:7]], axis=0)
        out.append((rows[t] + wide(shift[t]) * down) * wide(jnp.sqrt(square[t])))
    return jnp.concatenate(out, axis=0)


def factor_step(t_ref, step):
    s, e = step * PANEL, (step + 1) * PANEL
    new = eliminate_panel([t_ref[s + 8 * t : s + 8 * t + 8, :] for t in range(PANEL // 8)], s)
    if e < ROWS:
        n0, n1, n2 = split3(new)
        left = jnp.concatenate([n0, n0, n1, n1, n0, n2], axis=0)
        right = jnp.concatenate([n0, n1, n0, n1, n2, n0], axis=0)
        skip = e // 128 * 128
        update = lax.dot_general(left[:, skip:], right, (((0,), (0,)), ((), ())), preferred_element_type=f32)
        col = lax.broadcasted_iota(jnp.int32, (ROWS - e, ROWS), 1)
        t_ref[e:, :] = jnp.where((col >= s) & (col < e), 0.0, t_ref[e:, :]) - update[e - skip :]
    col = lax.broadcasted_iota(jnp.int32, (PANEL, ROWS), 1)
    t_ref[s:e, :] = jnp.where(col < e, new, 0.0)


def kernel(
    test_hbm, a_hbm, eofs_ref, pcs_ref,
    test_ref, a_ref, yown, yacc, basis, full, inv_ref, t_ref, norm_ref,
    wp, wc, ws, wf, r1, x2, x3,
    gp, g1, g2, g3, gf,
    test_sem, a_sem, y_ss, y_rs, wc_ss, wc_rs, w_ss, w_rs, gc_ss, gc_rs, g_ss, g_rs,
):
    space, y = lax.axis_index("space"), lax.axis_index("col")
    at = (space // 8, y, (space // 2) % 4)
    core = space % 2

    def peer(axis, d, across=0):
        x, yy, z = (((at[i] + d) % 4) if i == axis else at[i] for i in range(3))
        return ((x * 4 + z) * 2 + (core + across) % 2, yy)

    sibling = (space + 1 - 2 * core, y)

    def copy_to(device, src, dst, ss, rs):
        return pltpu.make_async_remote_copy(
            src_ref=src, dst_ref=dst, send_sem=ss, recv_sem=rs, device_id=device, device_id_type=MESH
        )

    def send(device, src, dst, ss, rs):
        copy = copy_to(device, src, dst, ss, rs)
        copy.start()
        return copy

    def points(i):
        return pl.ds(pl.multiple_of(OWN * i, OWN), OWN)

    load_test = pltpu.make_async_copy(test_hbm, test_ref, test_sem.at[0])
    load_test.start()
    blocks = [(y + d) % 4 for d in FAR_FIRST] + [y]
    loads = []
    for i, block in enumerate(blocks):
        for h in range(2):
            part = (pl.ds(h * (DAYS // 2), DAYS // 2), points(block))
            copy = pltpu.make_async_copy(a_hbm.at[part], a_ref.at[part], a_sem.at[i, h])
            copy.start()
            loads.append(copy)

    barrier = pltpu.get_barrier_semaphore()
    for axis in range(3):
        for d in FAR_FIRST:
            for across in (0, 1):
                pl.semaphore_signal(barrier, inc=1, device_id=peer(axis, d, across), device_id_type=MESH)
    pl.semaphore_signal(barrier, inc=1, device_id=sibling, device_id_type=MESH)

    load_test.wait()

    my_rows = pl.ds(pl.multiple_of(64 * y, 64), 64)
    first_copies = []
    for i, block in enumerate(blocks):
        loads[2 * i].wait()
        loads[2 * i + 1].wait()
        product = jnp.dot(test_ref[...], a_ref[:, points(block)], preferred_element_type=f32).astype(bf16)
        if i == 0:
            pl.semaphore_wait(barrier, 19)
        if i < 3:
            yown[i] = product
            first_copies.append(
                send(peer(1, FAR_FIRST[i]), yown.at[i], basis.at[my_rows, :], y_ss.at[i], y_rs.at[i])
            )
        else:
            basis[my_rows, :] = product
    for copy in first_copies:
        copy.wait()

    half = pl.ds(pl.multiple_of(128 * core, 128), 128)
    other = pl.ds(pl.multiple_of(128 * (1 - core), 128), 128)
    g_own = pl.multiple_of(192 * core, 64)
    g_other = pl.multiple_of(192 * (1 - core), 64)

    def order(g):
        return g % 3, (g + 1) % 3, (g + 2) % 3

    def days(u):
        return slice(STARTS[u], STARTS[u + 1])

    def rows_of(i):
        return pl.ds(pl.multiple_of(32 * i, 32), 32)

    def one_pass(k, carry):
        last = k == PASSES - 1
        now, before = k % 2, (k + 1) % 2
        def send_three(axis, pair, ss, rs, three):
            for d in FAR_FIRST:
                src, dst = pair(d)
                send(peer(axis, d), src, dst, ss, rs)
            return copy_to(sibling, three, three, ss, rs)

        def full_block(i):
            product = jnp.dot(
                wf[before], a_ref[:, i * OWN : (i + 1) * OWN], preferred_element_type=f32
            ).astype(bf16)
            full[:, i * OWN : (i + 1) * OWN] = (
                jnp.dot(inv_ref[...], product, preferred_element_type=f32) * (1.0 / POINTS)
            ).astype(bf16)

        gram = lax.dot_general(basis[...], basis[...], (((1,), (1,)), ((), ())), preferred_element_type=f32)
        gp[:ROWS, :] = gram[:, :128].astype(bf16)
        gp[ROWS:, :] = gram[128:, 128:].astype(bf16)

        w_core = []

        def product_unit(u):
            wp[:, days(u)] = lax.dot_general(
                basis[...], a_ref[days(u), points(y)], (((1,), (1,)), ((), ())), preferred_element_type=f32
            ).astype(bf16)
            w_core.append(send(sibling, wp.at[other, days(u)], wc.at[:, days(u)], wc_ss.at[0], wc_rs.at[0, u]))

        def gram_send(stage, buf, g, value):
            axis = order(g)[stage]
            mine = buf.at[g, at[axis]]
            mine[...] = value.astype(bf16)
            return send_three(axis, lambda d: (mine, mine), g_ss.at[stage], g_rs.at[stage, g], buf.at[g, 0:3])

        def gram_sum(arrived, buf, g):
            arrived.wait_recv()
            parts = [buf[g, i].astype(f32) for i in range(4)]
            return (parts[0] + parts[1]) + (parts[2] + parts[3])

        def four(buf, u):
            parts = [buf[u, i, :, : WIDTHS[u]].astype(f32) for i in range(4)]
            return ((parts[0] + parts[1]) + (parts[2] + parts[3])).astype(bf16)

        def slots(buf, u):
            return buf.at[u, 0:3, :, : WIDTHS[u]]

        ws1 = []

        def scatter(u):
            w_core[u].wait_recv()
            ws[:, days(u)] = (wp[half, days(u)].astype(f32) + wc[:, days(u)].astype(f32)).astype(bf16)
            axis = order(u)[0]
            ws1.append(
                send_three(
                    axis,
                    lambda d: (ws.at[rows_of((at[axis] + d) % 4), days(u)], r1.at[u, d - 1, :, : WIDTHS[u]]),
                    w_ss.at[0], w_rs.at[0, u], slots(r1, u),
                )
            )

        gs1 = []
        for g in range(3):
            slot = 4 * core + at[g]
            mine = gp.at[pl.ds(g_own + 64 * g, 64), :]
            theirs = gp.at[pl.ds(g_other + 64 * g, 64), :]
            for d in FAR_FIRST:
                send(peer(g, d, 1), theirs, g1.at[g, slot], g_ss.at[0], g_rs.at[0, g])
                send(peer(g, d), mine, g1.at[g, slot], g_ss.at[0], g_rs.at[0, g])
            send(sibling, theirs, g1.at[g, slot], g_ss.at[0], g_rs.at[0, g])
            g1[g, slot] = mine[...]
            gs1.append(copy_to(sibling, g1.at[g, 0:7], g1.at[g, 0:7], g_ss.at[0], g_rs.at[0, g]))

        for u in range(UNITS):
            product_unit(u)
            if u >= AHEAD:
                scatter(u - AHEAD)
        for u in range(UNITS - AHEAD, UNITS):
            scatter(u)

        @pl.when(last)
        def _():
            full_block(0)
            full_block(1)

        gs2 = []
        for g in range(3):
            gs1[g].wait_recv()
            parts = [g1[g, i].astype(f32) for i in range(8)]
            total = ((parts[0] + parts[1]) + (parts[2] + parts[3])) + ((parts[4] + parts[5]) + (parts[6] + parts[7]))
            gs2.append(gram_send(1, g2, g, total))

        ws2 = []
        for u in range(UNITS):
            ws1[u].wait_recv()
            first, axis, _ = order(u)
            total = ws[rows_of(at[first]), days(u)].astype(f32)
            for d in range(3):
                total += r1[u, d, :, : WIDTHS[u]].astype(f32)
            mine = x2.at[u, at[axis], :, : WIDTHS[u]]
            mine[...] = total.astype(bf16)
            ws2.append(send_three(axis, lambda d, m=mine: (m, m), w_ss.at[1], w_rs.at[1, u], slots(x2, u)))

        pl.when(last)(lambda: full_block(2))

        gs3 = [gram_send(2, g3, g, gram_sum(gs2[g], g2, g)) for g in range(3)]

        ws3 = []
        for u in range(UNITS):
            ws2[u].wait_recv()
            axis = order(u)[2]
            mine = x3.at[u, at[axis], :, : WIDTHS[u]]
            mine[...] = four(x2, u)
            ws3.append(send_three(axis, lambda d, m=mine: (m, m), w_ss.at[2], w_rs.at[2, u], slots(x3, u)))

        pl.when(last)(lambda: full_block(3))

        ws4, pieces = [], []

        def finish(u):
            ws3[u].wait_recv()
            piece = wf.at[now, rows_of(4 * core + at[order(u)[0]]), days(u)]
            piece[...] = four(x3, u)
            pieces.append(piece)

        def send_back(u):
            ws4.append(
                send_three(
                    order(u)[0], lambda d: (pieces[u], pieces[u]), w_ss.at[3], w_rs.at[3, u], slots(x3, u)
                )
            )

        for u in range(UNITS - 3):
            finish(u)
            send_back(u)
        for g in range(3):
            gf[pl.ds(g_own + 64 * g, 64), :] = gram_sum(gs3[g], g3, g)
        g_mine = gf.at[pl.ds(g_own, 192), :]
        g_back = send(sibling, g_mine, g_mine, gc_ss.at[1], gc_rs.at[1])
        for u in range(UNITS - 3, UNITS):
            finish(u)
        for u in range(UNITS - 3, UNITS):
            send_back(u)

        stage = wp.at[0:96, :]
        for i in range(3):
            copy_to(sibling, stage, stage, w_ss.at[i], w_rs.at[i, 0]).wait_send()
        for i, three in enumerate((g1.at[:, 0:7], g2.at[:, 0:3], g2.at[:, 0:3])):
            copy_to(sibling, three, three, g_ss.at[i], g_rs.at[i, 0]).wait_send()
        copy_to(sibling, wc, wc, wc_ss.at[0], wc_rs.at[0, 0]).wait_send()

        g_back.wait_recv()
        quarter = (128, 128)
        on = lax.broadcasted_iota(jnp.int32, quarter, 0) == lax.broadcasted_iota(jnp.int32, quarter, 1)
        upper, cross, lower = gf[:128, :], gf[128:ROWS, :], gf[ROWS:, :]
        diagonal = [jnp.where(on, upper, 0.0), jnp.where(on, lower, 0.0)]
        across = [lax.rsqrt(jnp.sum(v, axis=0, keepdims=True)) for v in diagonal]
        down = [lax.rsqrt(jnp.sum(v, axis=1, keepdims=True)) for v in diagonal]
        cross = cross * down[1] * across[0]
        t_ref[:128, :128] = upper * down[0] * across[0]
        t_ref[128:, 128:] = lower * down[1] * across[1]
        t_ref[128:, :128] = cross
        t_ref[:128, 128:] = cross.T
        norm_ref[...] = jnp.concatenate(across, axis=1) * POINTS**0.5

        w_back = []
        step = 0
        for what, n in SCHEDULE:
            if what == "factor":
                for _ in range(n):
                    factor_step(t_ref, step)
                    step += 1
            elif what == "share":
                for u in range(BATCHES[n], BATCHES[n + 1]):
                    ws4[u].wait_recv()
                    mine = wf.at[now, half, days(u)]
                    w_back.append(send(sibling, mine, mine, wc_ss.at[1], wc_rs.at[1, u]))
            else:
                for u in range(BATCHES[n], BATCHES[n + 1]):
                    w_back[u].wait_recv()
                own = slice(STARTS[BATCHES[n]], STARTS[BATCHES[n + 1]])
                product = jnp.dot(wf[now, :, own], a_ref[own, points(y)], preferred_element_type=f32)
                yacc[...] = product if n == 0 else yacc[...] + product
        inverse = (t_ref[...] * norm_ref[...]).astype(bf16)
        inv_ref[...] = inverse
        basis[...] = (
            jnp.dot(inverse, yacc[...].astype(bf16), preferred_element_type=f32) * (1.0 / POINTS)
        ).astype(bf16)

        copy_to(sibling, stage, stage, w_ss.at[3], w_rs.at[3, 0]).wait_send()
        copy_to(sibling, wc, wc, wc_ss.at[1], wc_rs.at[1, 0]).wait_send()
        g_back.wait_send()
        return carry

    lax.fori_loop(0, PASSES, one_pass, 0)

    own_inverse = inv_ref[my_rows, :]
    eofs_ref[...] = jnp.dot(own_inverse, full[...], preferred_element_type=f32)
    pcs_ref[...] = jnp.dot(own_inverse, wf[(PASSES - 1) % 2, :, :], preferred_element_type=f32) * (1.0 / POINTS)


def body(test_matrix, anomalies):
    vmem = pl.BlockSpec(memory_space=pltpu.VMEM)
    hbm = pl.BlockSpec(memory_space=pl.ANY)
    dma = pltpu.SemaphoreType.DMA
    return pl.pallas_call(
        kernel,
        out_shape=(jax.ShapeDtypeStruct((64, LOCAL), f32), jax.ShapeDtypeStruct((64, DAYS), f32)),
        in_specs=[hbm, hbm],
        out_specs=(vmem, vmem),
        scratch_shapes=[
            pltpu.VMEM((64, DAYS), bf16),
            pltpu.VMEM((DAYS, LOCAL), bf16),
            pltpu.VMEM((3, 64, OWN), bf16),
            pltpu.VMEM((ROWS, OWN), f32),
            pltpu.VMEM((ROWS, OWN), bf16),
            pltpu.VMEM((ROWS, LOCAL), bf16),
            pltpu.VMEM((ROWS, ROWS), bf16),
            pltpu.VMEM((ROWS, ROWS), f32),
            pltpu.VMEM((1, ROWS), f32),
            pltpu.VMEM((ROWS, DAYS), bf16),
            pltpu.VMEM((128, DAYS), bf16),
            pltpu.VMEM((128, DAYS), bf16),
            pltpu.VMEM((2, ROWS, DAYS), bf16),
            pltpu.VMEM((UNITS, 3, 32, WIDEST), bf16),
            pltpu.VMEM((UNITS, 4, 32, WIDEST), bf16),
            pltpu.VMEM((UNITS, 4, 32, WIDEST), bf16),
            pltpu.VMEM((384, 128), bf16),
            pltpu.VMEM((3, 8, 64, 128), bf16),
            pltpu.VMEM((3, 4, 64, 128), bf16),
            pltpu.VMEM((3, 4, 64, 128), bf16),
            pltpu.VMEM((384, 128), f32),
            dma((1,)),
            dma((4, 2)),
            dma((3,)),
            dma((3,)),
            dma((2,)),
            dma((2, UNITS)),
            dma((4,)),
            dma((4, UNITS)),
            dma((2,)),
            dma((2,)),
            dma((3,)),
            dma((3, 3)),
        ],
        compiler_params=pltpu.CompilerParams(collective_id=0, has_side_effects=True, vmem_limit_bytes=52 << 20),
        cost_estimate=pl.CostEstimate(flops=20 * 10**9, bytes_accessed=16 * 10**6, transcendentals=0),
        name="subspace_iteration",
    )(test_matrix, anomalies)


def solution(mesh):
    return jax.shard_map(
        body,
        mesh=mesh,
        in_specs=(P("col", None), P(None, "space")),
        out_specs=(P("col", "space"), P("col", None)),
        check_vma=False,
    )
```

```python
import jax
import jax.numpy as jnp
from jax import lax
from jax.experimental import pallas as pl
from jax.experimental.pallas import tpu as pltpu
from jax.sharding import PartitionSpec as P

f32, bf16 = jnp.float32, jnp.bfloat16
MESH = pl.DeviceIdType.MESH
PASSES = 3
ROWS, DAYS, POINTS = 256, 3712, 65536
LOCAL = 2048
OWN = 512
WIDTHS = [384] * 5 + [256] * 7
UNITS, WIDEST = len(WIDTHS), max(WIDTHS)
STARTS = [sum(WIDTHS[:u]) for u in range(UNITS + 1)]
BATCHES = (0, 6, 10, UNITS)
AHEAD = 4
PANEL, STRIP = 32, 16
FAR_FIRST = (2, 1, 3)
SCHEDULE = (
    ("gram", 0),
    ("back", 9),
    ("close", 0),
    ("build", 0),
    ("factor", 4),
    ("share", 6),
    ("share", 10),
    ("share", 12),
    ("factor", 2),
    ("use", 0),
    ("factor", 1),
    ("use", 1),
    ("use", 2),
    ("factor", 1),
)


def split3(a):
    first = a.astype(bf16)
    rest = a - first.astype(f32)
    second = rest.astype(bf16)
    return first, second, (rest - second.astype(f32)).astype(bf16)


def eliminate_panel(tiles, s):
    count = len(tiles)
    sub = lax.broadcasted_iota(jnp.int32, (8, 128), 0)
    sub_all = lax.broadcasted_iota(jnp.int32, (8, ROWS), 0)
    lane_all = lax.broadcasted_iota(jnp.int32, (8, ROWS), 1)
    rows = list(tiles)
    square, shift = [None] * count, [None] * count

    def spread(v, i):
        return jnp.broadcast_to(v[i : i + 1, :], v.shape)

    def wide(v):
        return jnp.concatenate([v, v], axis=1)

    for c0 in range(0, 8 * count, STRIP):
        q0, q1 = c0 // 8, (c0 + STRIP) // 8
        cols = [
            {
                t: jnp.broadcast_to(rows[t][:, s + c0 + c : s + c0 + c + 1], (8, 128))
                for t in range(q0 + c // 8, count)
            }
            for c in range(STRIP)
        ]
        inside = (lane_all >= s + c0) & (lane_all < s + c0 + STRIP)
        for t in range(count):
            unit = jnp.where(lane_all - s - 8 * t == sub_all, 1.0, 0.0) if q0 <= t < q1 else 0.0
            rows[t] = jnp.where(inside, unit, rows[t])
        for j in range(0, STRIP, 2):
            q, i = q0 + j // 8, j % 8
            x, y = cols[j], cols[j + 1]
            a, b, c = spread(x[q], i), spread(x[q], i + 1), spread(y[q], i + 1)
            over_a = 1.0 / a
            over_det = 1.0 / (a * c - b * b)
            an, bn, cn = a * over_det, b * over_det, c * over_det
            sq = jnp.where(sub == i, over_a, an)
            sh = jnp.where(sub == i + 1, -b * over_a, 0.0)
            square[q] = sq if i == 0 else jnp.where(sub >= i, sq, square[q])
            shift[q] = sh if i == 0 else jnp.where(sub >= i, sh, shift[q])
            first, second = spread(rows[q], i), spread(rows[q], i + 1)
            for t in range(q, count):
                u = cn * x[t] - bn * y[t]
                v = an * y[t] - bn * x[t]
                if t == q:
                    u = jnp.where(sub > i + 1, u, 0.0)
                    v = jnp.where(sub > i + 1, v, 0.0)
                for k in range(j + 2, STRIP):
                    tk = q0 + k // 8
                    if t >= tk:
                        cols[k][t] = cols[k][t] - u * spread(x[tk], k % 8) - v * spread(y[tk], k % 8)
                if t > q or i < 6:
                    rows[t] = rows[t] - wide(u) * first - wide(v) * second
    out = []
    for t in range(count):
        down = jnp.concatenate([rows[t][7:8], rows[t][0:7]], axis=0)
        out.append((rows[t] + wide(shift[t]) * down) * wide(jnp.sqrt(square[t])))
    return jnp.concatenate(out, axis=0)


def factor_step(t_ref, step):
    s, e = step * PANEL, (step + 1) * PANEL
    new = eliminate_panel([t_ref[s + 8 * t : s + 8 * t + 8, :] for t in range(PANEL // 8)], s)
    if e < ROWS:
        n0, n1, n2 = split3(new)
        left = jnp.concatenate([n0, n0, n1, n1, n0, n2], axis=0)
        right = jnp.concatenate([n0, n1, n0, n1, n2, n0], axis=0)
        skip = e // 128 * 128
        update = lax.dot_general(left[:, skip:], right, (((0,), (0,)), ((), ())), preferred_element_type=f32)
        col = lax.broadcasted_iota(jnp.int32, (ROWS - e, ROWS), 1)
        t_ref[e:, :] = jnp.where((col >= s) & (col < e), 0.0, t_ref[e:, :]) - update[e - skip :]
    col = lax.broadcasted_iota(jnp.int32, (PANEL, ROWS), 1)
    t_ref[s:e, :] = jnp.where(col < e, new, 0.0)


def kernel(
    test_hbm, a_hbm, eofs_ref, pcs_ref,
    test_ref, a_ref, yown, yacc, basis, full, inv_ref, t_ref, norm_ref,
    wp, wc, ws, wf, r1, x2, x3,
    gp, g1, g2, g3, gf,
    test_sem, a_sem, y_ss, y_rs, wc_ss, wc_rs, w_ss, w_rs, gc_ss, gc_rs, g_ss, g_rs,
):
    space, y = lax.axis_index("space"), lax.axis_index("col")
    at = (space // 8, y, (space // 2) % 4)
    core = space % 2

    def peer(axis, d, across=0):
        x, yy, z = (((at[i] + d) % 4) if i == axis else at[i] for i in range(3))
        return ((x * 4 + z) * 2 + (core + across) % 2, yy)

    sibling = (space + 1 - 2 * core, y)

    def copy_to(device, src, dst, ss, rs):
        return pltpu.make_async_remote_copy(
            src_ref=src, dst_ref=dst, send_sem=ss, recv_sem=rs, device_id=device, device_id_type=MESH
        )

    def send(device, src, dst, ss, rs):
        copy = copy_to(device, src, dst, ss, rs)
        copy.start()
        return copy

    def points(i):
        return pl.ds(pl.multiple_of(OWN * i, OWN), OWN)

    load_test = pltpu.make_async_copy(test_hbm, test_ref, test_sem.at[0])
    load_test.start()
    blocks = [(y + d) % 4 for d in FAR_FIRST] + [y]
    loads = []
    for i, block in enumerate(blocks):
        for h in range(2):
            part = (pl.ds(h * (DAYS // 2), DAYS // 2), points(block))
            copy = pltpu.make_async_copy(a_hbm.at[part], a_ref.at[part], a_sem.at[i, h])
            copy.start()
            loads.append(copy)

    barrier = pltpu.get_barrier_semaphore()
    for axis in range(3):
        for d in FAR_FIRST:
            for across in (0, 1):
                pl.semaphore_signal(barrier, inc=1, device_id=peer(axis, d, across), device_id_type=MESH)
    pl.semaphore_signal(barrier, inc=1, device_id=sibling, device_id_type=MESH)

    load_test.wait()

    my_rows = pl.ds(pl.multiple_of(64 * y, 64), 64)
    first_copies = []
    for i, block in enumerate(blocks):
        loads[2 * i].wait()
        loads[2 * i + 1].wait()
        product = jnp.dot(test_ref[...], a_ref[:, points(block)], preferred_element_type=f32).astype(bf16)
        if i == 0:
            pl.semaphore_wait(barrier, 19)
        if i < 3:
            yown[i] = product
            first_copies.append(
                send(peer(1, FAR_FIRST[i]), yown.at[i], basis.at[my_rows, :], y_ss.at[i], y_rs.at[i])
            )
        else:
            basis[my_rows, :] = product
    for copy in first_copies:
        copy.wait()

    half = pl.ds(pl.multiple_of(128 * core, 128), 128)
    other = pl.ds(pl.multiple_of(128 * (1 - core), 128), 128)
    g_own = pl.multiple_of(192 * core, 64)
    g_other = pl.multiple_of(192 * (1 - core), 64)

    def order(g):
        return g % 3, (g + 1) % 3, (g + 2) % 3

    def days(u):
        return slice(STARTS[u], STARTS[u + 1])

    def rows_of(i):
        return pl.ds(pl.multiple_of(32 * i, 32), 32)

    def one_pass(k, carry):
        last = k == PASSES - 1
        now, before = k % 2, (k + 1) % 2
        def send_three(axis, pair, ss, rs, three):
            for d in FAR_FIRST:
                src, dst = pair(d)
                send(peer(axis, d), src, dst, ss, rs)
            return copy_to(sibling, three, three, ss, rs)

        def full_block(d):
            block = points((y + d) % 4)
            product = jnp.dot(wf[before], a_ref[:, block], preferred_element_type=f32).astype(bf16)
            full[:, block] = (jnp.dot(inv_ref[...], product, preferred_element_type=f32) * (1.0 / POINTS)).astype(bf16)

        gram = lax.dot_general(basis[...], basis[...], (((1,), (1,)), ((), ())), preferred_element_type=f32)
        gp[:ROWS, :] = gram[:, :128].astype(bf16)
        gp[ROWS:, :] = gram[128:, 128:].astype(bf16)

        w_core = []

        def product_unit(u):
            wp[:, days(u)] = lax.dot_general(
                basis[...], a_ref[days(u), points(y)], (((1,), (1,)), ((), ())), preferred_element_type=f32
            ).astype(bf16)
            w_core.append(send(sibling, wp.at[other, days(u)], wc.at[:, days(u)], wc_ss.at[0], wc_rs.at[0, u]))

        def gram_send(stage, buf, g, value):
            axis = order(g)[stage]
            mine = buf.at[g, at[axis]]
            mine[...] = value.astype(bf16)
            return send_three(axis, lambda d: (mine, mine), g_ss.at[stage], g_rs.at[stage, g], buf.at[g, 0:3])

        def gram_sum(arrived, buf, g):
            arrived.wait_recv()
            parts = [buf[g, i].astype(f32) for i in range(4)]
            return (parts[0] + parts[1]) + (parts[2] + parts[3])

        def four(buf, u):
            parts = [buf[u, i, :, : WIDTHS[u]].astype(f32) for i in range(4)]
            return ((parts[0] + parts[1]) + (parts[2] + parts[3])).astype(bf16)

        def slots(buf, u):
            return buf.at[u, 0:3, :, : WIDTHS[u]]

        ws1 = []

        def scatter(u):
            w_core[u].wait_recv()
            ws[:, days(u)] = (wp[half, days(u)].astype(f32) + wc[:, days(u)].astype(f32)).astype(bf16)
            axis = order(u)[0]
            ws1.append(
                send_three(
                    axis,
                    lambda d: (ws.at[rows_of((at[axis] + d) % 4), days(u)], r1.at[u, d - 1, :, : WIDTHS[u]]),
                    w_ss.at[0], w_rs.at[0, u], slots(r1, u),
                )
            )

        gs1 = []
        for g in range(3):
            slot = 4 * core + at[g]
            mine = gp.at[pl.ds(g_own + 64 * g, 64), :]
            theirs = gp.at[pl.ds(g_other + 64 * g, 64), :]
            for d in FAR_FIRST:
                send(peer(g, d, 1), theirs, g1.at[g, slot], g_ss.at[0], g_rs.at[0, g])
                send(peer(g, d), mine, g1.at[g, slot], g_ss.at[0], g_rs.at[0, g])
            send(sibling, theirs, g1.at[g, slot], g_ss.at[0], g_rs.at[0, g])
            g1[g, slot] = mine[...]
            gs1.append(copy_to(sibling, g1.at[g, 0:7], g1.at[g, 0:7], g_ss.at[0], g_rs.at[0, g]))

        for u in range(UNITS):
            product_unit(u)
            if u >= AHEAD:
                scatter(u - AHEAD)
        for u in range(UNITS - AHEAD, UNITS):
            scatter(u)

        pl.when(last)(lambda: full_block(1))

        gs2 = []
        for g in range(3):
            gs1[g].wait_recv()
            parts = [g1[g, i].astype(f32) for i in range(8)]
            total = ((parts[0] + parts[1]) + (parts[2] + parts[3])) + ((parts[4] + parts[5]) + (parts[6] + parts[7]))
            gs2.append(gram_send(1, g2, g, total))

        ws2 = []
        for u in range(UNITS):
            ws1[u].wait_recv()
            first, axis, _ = order(u)
            total = ws[rows_of(at[first]), days(u)].astype(f32)
            for d in range(3):
                total += r1[u, d, :, : WIDTHS[u]].astype(f32)
            mine = x2.at[u, at[axis], :, : WIDTHS[u]]
            mine[...] = total.astype(bf16)
            ws2.append(send_three(axis, lambda d, m=mine: (m, m), w_ss.at[1], w_rs.at[1, u], slots(x2, u)))

        pl.when(last)(lambda: full_block(2))

        gs3 = [gram_send(2, g3, g, gram_sum(gs2[g], g2, g)) for g in range(3)]

        ws3 = []
        for u in range(UNITS):
            ws2[u].wait_recv()
            axis = order(u)[2]
            mine = x3.at[u, at[axis], :, : WIDTHS[u]]
            mine[...] = four(x2, u)
            ws3.append(send_three(axis, lambda d, m=mine: (m, m), w_ss.at[2], w_rs.at[2, u], slots(x3, u)))

        @pl.when(last)
        def _():
            full_block(3)
            full[:, points(y)] = basis[...]

        ws4, pieces = [], []

        def finish(u):
            ws3[u].wait_recv()
            piece = wf.at[now, rows_of(4 * core + at[order(u)[0]]), days(u)]
            piece[...] = four(x3, u)
            pieces.append(piece)

        def send_back(u):
            ws4.append(
                send_three(
                    order(u)[0], lambda d: (pieces[u], pieces[u]), w_ss.at[3], w_rs.at[3, u], slots(x3, u)
                )
            )

        def gram_back():
            for g in range(3):
                gf[pl.ds(g_own + 64 * g, 64), :] = gram_sum(gs3[g], g3, g)
            mine = gf.at[pl.ds(g_own, 192), :]
            return send(sibling, mine, mine, gc_ss.at[1], gc_rs.at[1])

        def build():
            g_back.wait_recv()
            quarter = (128, 128)
            on = lax.broadcasted_iota(jnp.int32, quarter, 0) == lax.broadcasted_iota(jnp.int32, quarter, 1)
            upper, cross, lower = gf[:128, :], gf[128:ROWS, :], gf[ROWS:, :]
            diagonal = [jnp.where(on, upper, 0.0), jnp.where(on, lower, 0.0)]
            across = [lax.rsqrt(jnp.sum(v, axis=0, keepdims=True)) for v in diagonal]
            down = [lax.rsqrt(jnp.sum(v, axis=1, keepdims=True)) for v in diagonal]
            cross = cross * down[1] * across[0]
            t_ref[:128, :128] = upper * down[0] * across[0]
            t_ref[128:, 128:] = lower * down[1] * across[1]
            t_ref[128:, :128] = cross
            t_ref[:128, 128:] = cross.T
            norm_ref[...] = jnp.concatenate(across, axis=1) * POINTS**0.5

        def share(u):
            ws4[u].wait_recv()
            mine = wf.at[now, half, days(u)]
            return send(sibling, mine, mine, wc_ss.at[1], wc_rs.at[1, u])

        def use(batch):
            for u in range(BATCHES[batch], BATCHES[batch + 1]):
                w_back[u].wait_recv()
            own = slice(STARTS[BATCHES[batch]], STARTS[BATCHES[batch + 1]])
            product = jnp.dot(wf[now, :, own], a_ref[own, points(y)], preferred_element_type=f32)
            yacc[...] = product if batch == 0 else yacc[...] + product

        w_back = []
        step = 0
        for what, n in SCHEDULE:
            if what == "gram":
                g_back = gram_back()
            elif what == "back":
                for u in range(len(pieces), n):
                    finish(u)
                    send_back(u)
            elif what == "close":
                for u in range(UNITS - 3, UNITS):
                    finish(u)
                for u in range(UNITS - 3, UNITS):
                    send_back(u)
            elif what == "build":
                build()
            elif what == "factor":
                for _ in range(n):
                    factor_step(t_ref, step)
                    step += 1
            elif what == "share":
                for u in range(len(w_back), n):
                    w_back.append(share(u))
            else:
                use(n)

        stage = wp.at[0:96, :]
        for i in range(3):
            copy_to(sibling, stage, stage, w_ss.at[i], w_rs.at[i, 0]).wait_send()
        for i, three in enumerate((g1.at[:, 0:7], g2.at[:, 0:3], g2.at[:, 0:3])):
            copy_to(sibling, three, three, g_ss.at[i], g_rs.at[i, 0]).wait_send()
        copy_to(sibling, wc, wc, wc_ss.at[0], wc_rs.at[0, 0]).wait_send()

        inverse = (t_ref[...] * norm_ref[...]).astype(bf16)
        inv_ref[...] = inverse
        basis[...] = (
            jnp.dot(inverse, yacc[...].astype(bf16), preferred_element_type=f32) * (1.0 / POINTS)
        ).astype(bf16)

        copy_to(sibling, stage, stage, w_ss.at[3], w_rs.at[3, 0]).wait_send()
        copy_to(sibling, wc, wc, wc_ss.at[1], wc_rs.at[1, 0]).wait_send()
        g_back.wait_send()
        return carry

    lax.fori_loop(0, PASSES, one_pass, 0)

    own_inverse = inv_ref[my_rows, :]
    eofs_ref[...] = jnp.dot(own_inverse, full[...], preferred_element_type=f32)
    pcs_ref[...] = jnp.dot(own_inverse, wf[(PASSES - 1) % 2, :, :], preferred_element_type=f32) * (1.0 / POINTS)


def body(test_matrix, anomalies):
    vmem = pl.BlockSpec(memory_space=pltpu.VMEM)
    hbm = pl.BlockSpec(memory_space=pl.ANY)
    dma = pltpu.SemaphoreType.DMA
    return pl.pallas_call(
        kernel,
        out_shape=(jax.ShapeDtypeStruct((64, LOCAL), f32), jax.ShapeDtypeStruct((64, DAYS), f32)),
        in_specs=[hbm, hbm],
        out_specs=(vmem, vmem),
        scratch_shapes=[
            pltpu.VMEM((64, DAYS), bf16),
            pltpu.VMEM((DAYS, LOCAL), bf16),
            pltpu.VMEM((3, 64, OWN), bf16),
            pltpu.VMEM((ROWS, OWN), f32),
            pltpu.VMEM((ROWS, OWN), bf16),
            pltpu.VMEM((ROWS, LOCAL), bf16),
            pltpu.VMEM((ROWS, ROWS), bf16),
            pltpu.VMEM((ROWS, ROWS), f32),
            pltpu.VMEM((1, ROWS), f32),
            pltpu.VMEM((ROWS, DAYS), bf16),
            pltpu.VMEM((128, DAYS), bf16),
            pltpu.VMEM((128, DAYS), bf16),
            pltpu.VMEM((2, ROWS, DAYS), bf16),
            pltpu.VMEM((UNITS, 3, 32, WIDEST), bf16),
            pltpu.VMEM((UNITS, 4, 32, WIDEST), bf16),
            pltpu.VMEM((UNITS, 4, 32, WIDEST), bf16),
            pltpu.VMEM((384, 128), bf16),
            pltpu.VMEM((3, 8, 64, 128), bf16),
            pltpu.VMEM((3, 4, 64, 128), bf16),
            pltpu.VMEM((3, 4, 64, 128), bf16),
            pltpu.VMEM((384, 128), f32),
            dma((1,)),
            dma((4, 2)),
            dma((3,)),
            dma((3,)),
            dma((2,)),
            dma((2, UNITS)),
            dma((4,)),
            dma((4, UNITS)),
            dma((2,)),
            dma((2,)),
            dma((3,)),
            dma((3, 3)),
        ],
        compiler_params=pltpu.CompilerParams(collective_id=0, has_side_effects=True, vmem_limit_bytes=52 << 20),
        cost_estimate=pl.CostEstimate(flops=20 * 10**9, bytes_accessed=16 * 10**6, transcendentals=0),
        name="subspace_iteration",
    )(test_matrix, anomalies)


def solution(mesh):
    return jax.shard_map(
        body,
        mesh=mesh,
        in_specs=(P("col", None), P(None, "space")),
        out_specs=(P("col", "space"), P("col", None)),
        check_vma=False,
    )
```

```python
import jax
import jax.numpy as jnp
from jax import lax
from jax.experimental import pallas as pl
from jax.experimental.pallas import tpu as pltpu
from jax.sharding import PartitionSpec as P

f32, bf16 = jnp.float32, jnp.bfloat16
MESH = pl.DeviceIdType.MESH
PASSES = 3
ROWS, DAYS, POINTS = 256, 3712, 65536
LOCAL = 2048
OWN = 512
WIDTHS = [512] * 2 + [384] * 7
UNITS, WIDEST = len(WIDTHS), max(WIDTHS)
STARTS = [sum(WIDTHS[:u]) for u in range(UNITS + 1)]
BATCHES = (0, 4, 7, UNITS)
AHEAD = 4
PANEL, STRIP = 32, 16
FAR_FIRST = (2, 1, 3)
SCHEDULE = (
    ("gram", 0),
    ("back", 6),
    ("close", 0),
    ("build", 0),
    ("factor", 4),
    ("share", 4),
    ("share", 7),
    ("share", 9),
    ("factor", 2),
    ("use", 0),
    ("factor", 1),
    ("use", 1),
    ("use", 2),
    ("factor", 1),
)


def split3(a):
    first = a.astype(bf16)
    rest = a - first.astype(f32)
    second = rest.astype(bf16)
    return first, second, (rest - second.astype(f32)).astype(bf16)


def eliminate_panel(tiles, s):
    count = len(tiles)
    sub = lax.broadcasted_iota(jnp.int32, (8, 128), 0)
    sub_all = lax.broadcasted_iota(jnp.int32, (8, ROWS), 0)
    lane_all = lax.broadcasted_iota(jnp.int32, (8, ROWS), 1)
    rows = list(tiles)
    square, shift = [None] * count, [None] * count

    def spread(v, i):
        return jnp.broadcast_to(v[i : i + 1, :], v.shape)

    def wide(v):
        return jnp.concatenate([v, v], axis=1)

    for c0 in range(0, 8 * count, STRIP):
        q0, q1 = c0 // 8, (c0 + STRIP) // 8
        cols = [
            {
                t: jnp.broadcast_to(rows[t][:, s + c0 + c : s + c0 + c + 1], (8, 128))
                for t in range(q0 + c // 8, count)
            }
            for c in range(STRIP)
        ]
        inside = (lane_all >= s + c0) & (lane_all < s + c0 + STRIP)
        for t in range(count):
            unit = jnp.where(lane_all - s - 8 * t == sub_all, 1.0, 0.0) if q0 <= t < q1 else 0.0
            rows[t] = jnp.where(inside, unit, rows[t])
        for j in range(0, STRIP, 2):
            q, i = q0 + j // 8, j % 8
            x, y = cols[j], cols[j + 1]
            a, b, c = spread(x[q], i), spread(x[q], i + 1), spread(y[q], i + 1)
            over_a = 1.0 / a
            over_det = 1.0 / (a * c - b * b)
            an, bn, cn = a * over_det, b * over_det, c * over_det
            sq = jnp.where(sub == i, over_a, an)
            sh = jnp.where(sub == i + 1, -b * over_a, 0.0)
            square[q] = sq if i == 0 else jnp.where(sub >= i, sq, square[q])
            shift[q] = sh if i == 0 else jnp.where(sub >= i, sh, shift[q])
            first, second = spread(rows[q], i), spread(rows[q], i + 1)
            for t in range(q, count):
                u = cn * x[t] - bn * y[t]
                v = an * y[t] - bn * x[t]
                if t == q:
                    u = jnp.where(sub > i + 1, u, 0.0)
                    v = jnp.where(sub > i + 1, v, 0.0)
                for k in range(j + 2, STRIP):
                    tk = q0 + k // 8
                    if t >= tk:
                        cols[k][t] = cols[k][t] - u * spread(x[tk], k % 8) - v * spread(y[tk], k % 8)
                if t > q or i < 6:
                    rows[t] = rows[t] - wide(u) * first - wide(v) * second
    out = []
    for t in range(count):
        down = jnp.concatenate([rows[t][7:8], rows[t][0:7]], axis=0)
        out.append((rows[t] + wide(shift[t]) * down) * wide(jnp.sqrt(square[t])))
    return jnp.concatenate(out, axis=0)


def factor_step(t_ref, step):
    s, e = step * PANEL, (step + 1) * PANEL
    new = eliminate_panel([t_ref[s + 8 * t : s + 8 * t + 8, :] for t in range(PANEL // 8)], s)
    if e < ROWS:
        n0, n1, n2 = split3(new)
        left = jnp.concatenate([n0, n0, n1, n1, n0, n2], axis=0)
        right = jnp.concatenate([n0, n1, n0, n1, n2, n0], axis=0)
        skip = e // 128 * 128
        update = lax.dot_general(left[:, skip:], right, (((0,), (0,)), ((), ())), preferred_element_type=f32)
        col = lax.broadcasted_iota(jnp.int32, (ROWS - e, ROWS), 1)
        t_ref[e:, :] = jnp.where((col >= s) & (col < e), 0.0, t_ref[e:, :]) - update[e - skip :]
    col = lax.broadcasted_iota(jnp.int32, (PANEL, ROWS), 1)
    t_ref[s:e, :] = jnp.where(col < e, new, 0.0)


def kernel(
    test_hbm, a_hbm, eofs_ref, pcs_ref,
    test_ref, a_ref, yown, yacc, basis, full, inv_ref, t_ref, norm_ref,
    wp, wc, ws, wf, r1, x2, x3,
    gp, g1, g2, g3, gf,
    test_sem, a_sem, y_ss, y_rs, wc_ss, wc_rs, w_ss, w_rs, gc_ss, gc_rs, g_ss, g_rs,
):
    space, y = lax.axis_index("space"), lax.axis_index("col")
    at = (space // 8, y, (space // 2) % 4)
    core = space % 2

    def peer(axis, d, across=0):
        x, yy, z = (((at[i] + d) % 4) if i == axis else at[i] for i in range(3))
        return ((x * 4 + z) * 2 + (core + across) % 2, yy)

    sibling = (space + 1 - 2 * core, y)

    def copy_to(device, src, dst, ss, rs):
        return pltpu.make_async_remote_copy(
            src_ref=src, dst_ref=dst, send_sem=ss, recv_sem=rs, device_id=device, device_id_type=MESH
        )

    def send(device, src, dst, ss, rs):
        copy = copy_to(device, src, dst, ss, rs)
        copy.start()
        return copy

    def points(i):
        return pl.ds(pl.multiple_of(OWN * i, OWN), OWN)

    load_test = pltpu.make_async_copy(test_hbm, test_ref, test_sem.at[0])
    load_test.start()
    blocks = [(y + d) % 4 for d in FAR_FIRST] + [y]
    loads = []
    for i, block in enumerate(blocks):
        for h in range(2):
            part = (pl.ds(h * (DAYS // 2), DAYS // 2), points(block))
            copy = pltpu.make_async_copy(a_hbm.at[part], a_ref.at[part], a_sem.at[i, h])
            copy.start()
            loads.append(copy)

    barrier = pltpu.get_barrier_semaphore()
    for axis in range(3):
        for d in FAR_FIRST:
            for across in (0, 1):
                pl.semaphore_signal(barrier, inc=1, device_id=peer(axis, d, across), device_id_type=MESH)
    pl.semaphore_signal(barrier, inc=1, device_id=sibling, device_id_type=MESH)

    load_test.wait()

    my_rows = pl.ds(pl.multiple_of(64 * y, 64), 64)
    first_copies = []
    for i, block in enumerate(blocks):
        loads[2 * i].wait()
        loads[2 * i + 1].wait()
        product = jnp.dot(test_ref[...], a_ref[:, points(block)], preferred_element_type=f32).astype(bf16)
        if i == 0:
            pl.semaphore_wait(barrier, 19)
        if i < 3:
            yown[i] = product
            first_copies.append(
                send(peer(1, FAR_FIRST[i]), yown.at[i], basis.at[my_rows, :], y_ss.at[i], y_rs.at[i])
            )
        else:
            basis[my_rows, :] = product
    for copy in first_copies:
        copy.wait()

    half = pl.ds(pl.multiple_of(128 * core, 128), 128)
    other = pl.ds(pl.multiple_of(128 * (1 - core), 128), 128)
    g_own = pl.multiple_of(192 * core, 64)
    g_other = pl.multiple_of(192 * (1 - core), 64)

    def order(g):
        return g % 3, (g + 1) % 3, (g + 2) % 3

    def days(u):
        return slice(STARTS[u], STARTS[u + 1])

    def rows_of(i):
        return pl.ds(pl.multiple_of(32 * i, 32), 32)

    def one_pass(k, carry):
        last = k == PASSES - 1
        now, before = k % 2, (k + 1) % 2
        def send_three(axis, pair, ss, rs, three):
            for d in FAR_FIRST:
                src, dst = pair(d)
                send(peer(axis, d), src, dst, ss, rs)
            return copy_to(sibling, three, three, ss, rs)

        def full_block(d):
            block = points((y + d) % 4)
            product = jnp.dot(wf[before], a_ref[:, block], preferred_element_type=f32).astype(bf16)
            full[:, block] = (jnp.dot(inv_ref[...], product, preferred_element_type=f32) * (1.0 / POINTS)).astype(bf16)

        gram = lax.dot_general(basis[...], basis[...], (((1,), (1,)), ((), ())), preferred_element_type=f32)
        gp[:ROWS, :] = gram[:, :128].astype(bf16)
        gp[ROWS:, :] = gram[128:, 128:].astype(bf16)

        w_core = []

        def product_unit(u):
            wp[:, days(u)] = lax.dot_general(
                basis[...], a_ref[days(u), points(y)], (((1,), (1,)), ((), ())), preferred_element_type=f32
            ).astype(bf16)
            w_core.append(send(sibling, wp.at[other, days(u)], wc.at[:, days(u)], wc_ss.at[0], wc_rs.at[0, u]))

        def gram_send(stage, buf, g, value):
            axis = order(g)[stage]
            mine = buf.at[g, at[axis]]
            mine[...] = value.astype(bf16)
            return send_three(axis, lambda d: (mine, mine), g_ss.at[stage], g_rs.at[stage, g], buf.at[g, 0:3])

        def gram_sum(arrived, buf, g):
            arrived.wait_recv()
            parts = [buf[g, i].astype(f32) for i in range(4)]
            return (parts[0] + parts[1]) + (parts[2] + parts[3])

        def four(buf, u):
            parts = [buf[u, i, :, : WIDTHS[u]].astype(f32) for i in range(4)]
            return ((parts[0] + parts[1]) + (parts[2] + parts[3])).astype(bf16)

        def slots(buf, u):
            return buf.at[u, 0:3, :, : WIDTHS[u]]

        ws1 = []

        def scatter(u):
            w_core[u].wait_recv()
            ws[:, days(u)] = (wp[half, days(u)].astype(f32) + wc[:, days(u)].astype(f32)).astype(bf16)
            axis = order(u)[0]
            ws1.append(
                send_three(
                    axis,
                    lambda d: (ws.at[rows_of((at[axis] + d) % 4), days(u)], r1.at[u, d - 1, :, : WIDTHS[u]]),
                    w_ss.at[0], w_rs.at[0, u], slots(r1, u),
                )
            )

        gs1 = []
        for g in range(3):
            slot = 4 * core + at[g]
            mine = gp.at[pl.ds(g_own + 64 * g, 64), :]
            theirs = gp.at[pl.ds(g_other + 64 * g, 64), :]
            for d in FAR_FIRST:
                send(peer(g, d, 1), theirs, g1.at[g, slot], g_ss.at[0], g_rs.at[0, g])
                send(peer(g, d), mine, g1.at[g, slot], g_ss.at[0], g_rs.at[0, g])
            send(sibling, theirs, g1.at[g, slot], g_ss.at[0], g_rs.at[0, g])
            g1[g, slot] = mine[...]
            gs1.append(copy_to(sibling, g1.at[g, 0:7], g1.at[g, 0:7], g_ss.at[0], g_rs.at[0, g]))

        for u in range(UNITS):
            product_unit(u)
            if u >= AHEAD:
                scatter(u - AHEAD)
        for u in range(UNITS - AHEAD, UNITS):
            scatter(u)

        pl.when(last)(lambda: full_block(1))

        gs2 = []
        for g in range(3):
            gs1[g].wait_recv()
            parts = [g1[g, i].astype(f32) for i in range(8)]
            total = ((parts[0] + parts[1]) + (parts[2] + parts[3])) + ((parts[4] + parts[5]) + (parts[6] + parts[7]))
            gs2.append(gram_send(1, g2, g, total))

        ws2 = []
        for u in range(UNITS):
            ws1[u].wait_recv()
            first, axis, _ = order(u)
            total = ws[rows_of(at[first]), days(u)].astype(f32)
            for d in range(3):
                total += r1[u, d, :, : WIDTHS[u]].astype(f32)
            mine = x2.at[u, at[axis], :, : WIDTHS[u]]
            mine[...] = total.astype(bf16)
            ws2.append(send_three(axis, lambda d, m=mine: (m, m), w_ss.at[1], w_rs.at[1, u], slots(x2, u)))

        pl.when(last)(lambda: full_block(2))

        gs3 = [gram_send(2, g3, g, gram_sum(gs2[g], g2, g)) for g in range(3)]

        ws3 = []
        for u in range(UNITS):
            ws2[u].wait_recv()
            axis = order(u)[2]
            mine = x3.at[u, at[axis], :, : WIDTHS[u]]
            mine[...] = four(x2, u)
            ws3.append(send_three(axis, lambda d, m=mine: (m, m), w_ss.at[2], w_rs.at[2, u], slots(x3, u)))

        @pl.when(last)
        def _():
            full_block(3)
            full[:, points(y)] = basis[...]

        ws4, pieces = [], []

        def finish(u):
            ws3[u].wait_recv()
            piece = wf.at[now, rows_of(4 * core + at[order(u)[0]]), days(u)]
            piece[...] = four(x3, u)
            pieces.append(piece)

        def send_back(u):
            ws4.append(
                send_three(
                    order(u)[0], lambda d: (pieces[u], pieces[u]), w_ss.at[3], w_rs.at[3, u], slots(x3, u)
                )
            )

        def gram_back():
            for g in range(3):
                gf[pl.ds(g_own + 64 * g, 64), :] = gram_sum(gs3[g], g3, g)
            mine = gf.at[pl.ds(g_own, 192), :]
            return send(sibling, mine, mine, gc_ss.at[1], gc_rs.at[1])

        def build():
            g_back.wait_recv()
            quarter = (128, 128)
            on = lax.broadcasted_iota(jnp.int32, quarter, 0) == lax.broadcasted_iota(jnp.int32, quarter, 1)
            upper, cross, lower = gf[:128, :], gf[128:ROWS, :], gf[ROWS:, :]
            diagonal = [jnp.where(on, upper, 0.0), jnp.where(on, lower, 0.0)]
            across = [lax.rsqrt(jnp.sum(v, axis=0, keepdims=True)) for v in diagonal]
            down = [lax.rsqrt(jnp.sum(v, axis=1, keepdims=True)) for v in diagonal]
            cross = cross * down[1] * across[0]
            t_ref[:128, :128] = upper * down[0] * across[0]
            t_ref[128:, 128:] = lower * down[1] * across[1]
            t_ref[128:, :128] = cross
            t_ref[:128, 128:] = cross.T
            norm_ref[...] = jnp.concatenate(across, axis=1) * POINTS**0.5

        def share(u):
            ws4[u].wait_recv()
            mine = wf.at[now, half, days(u)]
            return send(sibling, mine, mine, wc_ss.at[1], wc_rs.at[1, u])

        def use(batch):
            for u in range(BATCHES[batch], BATCHES[batch + 1]):
                w_back[u].wait_recv()
            own = slice(STARTS[BATCHES[batch]], STARTS[BATCHES[batch + 1]])
            product = jnp.dot(wf[now, :, own], a_ref[own, points(y)], preferred_element_type=f32)
            yacc[...] = product if batch == 0 else yacc[...] + product

        w_back = []
        step = 0
        for what, n in SCHEDULE:
            if what == "gram":
                g_back = gram_back()
            elif what == "back":
                for u in range(len(pieces), n):
                    finish(u)
                    send_back(u)
            elif what == "close":
                for u in range(UNITS - 3, UNITS):
                    finish(u)
                for u in range(UNITS - 3, UNITS):
                    send_back(u)
            elif what == "build":
                build()
            elif what == "factor":
                for _ in range(n):
                    factor_step(t_ref, step)
                    step += 1
            elif what == "share":
                for u in range(len(w_back), n):
                    w_back.append(share(u))
            else:
                use(n)

        stage = wp.at[0:96, :]
        for i in range(3):
            copy_to(sibling, stage, stage, w_ss.at[i], w_rs.at[i, 0]).wait_send()
        for i, three in enumerate((g1.at[:, 0:7], g2.at[:, 0:3], g2.at[:, 0:3])):
            copy_to(sibling, three, three, g_ss.at[i], g_rs.at[i, 0]).wait_send()
        copy_to(sibling, wc, wc, wc_ss.at[0], wc_rs.at[0, 0]).wait_send()

        inverse = (t_ref[...] * norm_ref[...]).astype(bf16)
        inv_ref[...] = inverse
        basis[...] = (
            jnp.dot(inverse, yacc[...].astype(bf16), preferred_element_type=f32) * (1.0 / POINTS)
        ).astype(bf16)

        copy_to(sibling, stage, stage, w_ss.at[3], w_rs.at[3, 0]).wait_send()
        copy_to(sibling, wc, wc, wc_ss.at[1], wc_rs.at[1, 0]).wait_send()
        g_back.wait_send()
        return carry

    lax.fori_loop(0, PASSES, one_pass, 0)

    own_inverse = inv_ref[my_rows, :]
    eofs_ref[...] = jnp.dot(own_inverse, full[...], preferred_element_type=f32)
    pcs_ref[...] = jnp.dot(own_inverse, wf[(PASSES - 1) % 2, :, :], preferred_element_type=f32) * (1.0 / POINTS)


def body(test_matrix, anomalies):
    vmem = pl.BlockSpec(memory_space=pltpu.VMEM)
    hbm = pl.BlockSpec(memory_space=pl.ANY)
    dma = pltpu.SemaphoreType.DMA
    return pl.pallas_call(
        kernel,
        out_shape=(jax.ShapeDtypeStruct((64, LOCAL), f32), jax.ShapeDtypeStruct((64, DAYS), f32)),
        in_specs=[hbm, hbm],
        out_specs=(vmem, vmem),
        scratch_shapes=[
            pltpu.VMEM((64, DAYS), bf16),
            pltpu.VMEM((DAYS, LOCAL), bf16),
            pltpu.VMEM((3, 64, OWN), bf16),
            pltpu.VMEM((ROWS, OWN), f32),
            pltpu.VMEM((ROWS, OWN), bf16),
            pltpu.VMEM((ROWS, LOCAL), bf16),
            pltpu.VMEM((ROWS, ROWS), bf16),
            pltpu.VMEM((ROWS, ROWS), f32),
            pltpu.VMEM((1, ROWS), f32),
            pltpu.VMEM((ROWS, DAYS), bf16),
            pltpu.VMEM((128, DAYS), bf16),
            pltpu.VMEM((128, DAYS), bf16),
            pltpu.VMEM((2, ROWS, DAYS), bf16),
            pltpu.VMEM((UNITS, 3, 32, WIDEST), bf16),
            pltpu.VMEM((UNITS, 4, 32, WIDEST), bf16),
            pltpu.VMEM((UNITS, 4, 32, WIDEST), bf16),
            pltpu.VMEM((384, 128), bf16),
            pltpu.VMEM((3, 8, 64, 128), bf16),
            pltpu.VMEM((3, 4, 64, 128), bf16),
            pltpu.VMEM((3, 4, 64, 128), bf16),
            pltpu.VMEM((384, 128), f32),
            dma((1,)),
            dma((4, 2)),
            dma((3,)),
            dma((3,)),
            dma((2,)),
            dma((2, UNITS)),
            dma((4,)),
            dma((4, UNITS)),
            dma((2,)),
            dma((2,)),
            dma((3,)),
            dma((3, 3)),
        ],
        compiler_params=pltpu.CompilerParams(collective_id=0, has_side_effects=True, vmem_limit_bytes=52 << 20),
        cost_estimate=pl.CostEstimate(flops=20 * 10**9, bytes_accessed=16 * 10**6, transcendentals=0),
        name="subspace_iteration",
    )(test_matrix, anomalies)


def solution(mesh):
    return jax.shard_map(
        body,
        mesh=mesh,
        in_specs=(P("col", None), P(None, "space")),
        out_specs=(P("col", "space"), P("col", None)),
        check_vma=False,
    )
```

```python
import jax
import jax.numpy as jnp
from jax import lax
from jax.experimental import pallas as pl
from jax.experimental.pallas import tpu as pltpu
from jax.sharding import PartitionSpec as P

f32, bf16 = jnp.float32, jnp.bfloat16
MESH = pl.DeviceIdType.MESH
PASSES = 3
ROWS, DAYS, POINTS = 256, 3712, 65536
LOCAL = 2048
OWN = 512
WIDTHS = [512] * 2 + [384] * 7
UNITS, WIDEST = len(WIDTHS), max(WIDTHS)
STARTS = [sum(WIDTHS[:u]) for u in range(UNITS + 1)]
BATCHES = (0, 4, 7, UNITS)
AHEAD = 3
PANEL, STRIP = 32, 16
FAR_FIRST = (2, 1, 3)
SCHEDULE = (
    ("gram", 0),
    ("back", 6),
    ("close", 0),
    ("build", 0),
    ("factor", 4),
    ("share", 4),
    ("share", 7),
    ("share", 9),
    ("factor", 2),
    ("use", 0),
    ("factor", 1),
    ("use", 1),
    ("use", 2),
    ("factor", 1),
)


def split3(a):
    first = a.astype(bf16)
    rest = a - first.astype(f32)
    second = rest.astype(bf16)
    return first, second, (rest - second.astype(f32)).astype(bf16)


def eliminate_panel(tiles, s):
    count = len(tiles)
    sub = lax.broadcasted_iota(jnp.int32, (8, 128), 0)
    sub_all = lax.broadcasted_iota(jnp.int32, (8, ROWS), 0)
    lane_all = lax.broadcasted_iota(jnp.int32, (8, ROWS), 1)
    rows = list(tiles)
    square, shift = [None] * count, [None] * count

    def spread(v, i):
        return jnp.broadcast_to(v[i : i + 1, :], v.shape)

    def wide(v):
        return jnp.concatenate([v, v], axis=1)

    for c0 in range(0, 8 * count, STRIP):
        q0, q1 = c0 // 8, (c0 + STRIP) // 8
        cols = [
            {
                t: jnp.broadcast_to(rows[t][:, s + c0 + c : s + c0 + c + 1], (8, 128))
                for t in range(q0 + c // 8, count)
            }
            for c in range(STRIP)
        ]
        inside = (lane_all >= s + c0) & (lane_all < s + c0 + STRIP)
        for t in range(count):
            unit = jnp.where(lane_all - s - 8 * t == sub_all, 1.0, 0.0) if q0 <= t < q1 else 0.0
            rows[t] = jnp.where(inside, unit, rows[t])
        for j in range(0, STRIP, 2):
            q, i = q0 + j // 8, j % 8
            x, y = cols[j], cols[j + 1]
            a, b, c = spread(x[q], i), spread(x[q], i + 1), spread(y[q], i + 1)
            over_a = 1.0 / a
            over_det = 1.0 / (a * c - b * b)
            an, bn, cn = a * over_det, b * over_det, c * over_det
            sq = jnp.where(sub == i, over_a, an)
            sh = jnp.where(sub == i + 1, -b * over_a, 0.0)
            square[q] = sq if i == 0 else jnp.where(sub >= i, sq, square[q])
            shift[q] = sh if i == 0 else jnp.where(sub >= i, sh, shift[q])
            first, second = spread(rows[q], i), spread(rows[q], i + 1)
            for t in range(q, count):
                u = cn * x[t] - bn * y[t]
                v = an * y[t] - bn * x[t]
                if t == q:
                    u = jnp.where(sub > i + 1, u, 0.0)
                    v = jnp.where(sub > i + 1, v, 0.0)
                for k in range(j + 2, STRIP):
                    tk = q0 + k // 8
                    if t >= tk:
                        cols[k][t] = cols[k][t] - u * spread(x[tk], k % 8) - v * spread(y[tk], k % 8)
                if t > q or i < 6:
                    rows[t] = rows[t] - wide(u) * first - wide(v) * second
    out = []
    for t in range(count):
        down = jnp.concatenate([rows[t][7:8], rows[t][0:7]], axis=0)
        out.append((rows[t] + wide(shift[t]) * down) * wide(jnp.sqrt(square[t])))
    return jnp.concatenate(out, axis=0)


def factor_step(t_ref, step):
    s, e = step * PANEL, (step + 1) * PANEL
    new = eliminate_panel([t_ref[s + 8 * t : s + 8 * t + 8, :] for t in range(PANEL // 8)], s)
    if e < ROWS:
        n0, n1, n2 = split3(new)
        left = jnp.concatenate([n0, n0, n1, n1, n0, n2], axis=0)
        right = jnp.concatenate([n0, n1, n0, n1, n2, n0], axis=0)
        skip = e // 128 * 128
        update = lax.dot_general(left[:, skip:], right, (((0,), (0,)), ((), ())), preferred_element_type=f32)
        col = lax.broadcasted_iota(jnp.int32, (ROWS - e, ROWS), 1)
        t_ref[e:, :] = jnp.where((col >= s) & (col < e), 0.0, t_ref[e:, :]) - update[e - skip :]
    col = lax.broadcasted_iota(jnp.int32, (PANEL, ROWS), 1)
    t_ref[s:e, :] = jnp.where(col < e, new, 0.0)


def kernel(
    test_hbm, a_hbm, eofs_ref, pcs_ref,
    test_ref, a_ref, yown, yacc, basis, full, inv_ref, t_ref, norm_ref,
    wp, wc, ws, wf, r1, x2, x3,
    gp, g1, g2, g3, gf,
    test_sem, a_sem, y_ss, y_rs, wc_ss, wc_rs, w_ss, w_rs, gc_ss, gc_rs, g_ss, g_rs,
):
    space, y = lax.axis_index("space"), lax.axis_index("col")
    at = (space // 8, y, (space // 2) % 4)
    core = space % 2

    def peer(axis, d, across=0):
        x, yy, z = (((at[i] + d) % 4) if i == axis else at[i] for i in range(3))
        return ((x * 4 + z) * 2 + (core + across) % 2, yy)

    sibling = (space + 1 - 2 * core, y)

    def copy_to(device, src, dst, ss, rs):
        return pltpu.make_async_remote_copy(
            src_ref=src, dst_ref=dst, send_sem=ss, recv_sem=rs, device_id=device, device_id_type=MESH
        )

    def send(device, src, dst, ss, rs):
        copy = copy_to(device, src, dst, ss, rs)
        copy.start()
        return copy

    def points(i):
        return pl.ds(pl.multiple_of(OWN * i, OWN), OWN)

    load_test = pltpu.make_async_copy(test_hbm, test_ref, test_sem.at[0])
    load_test.start()
    blocks = [(y + d) % 4 for d in FAR_FIRST] + [y]
    loads = []
    for i, block in enumerate(blocks):
        for h in range(2):
            part = (pl.ds(h * (DAYS // 2), DAYS // 2), points(block))
            copy = pltpu.make_async_copy(a_hbm.at[part], a_ref.at[part], a_sem.at[i, h])
            copy.start()
            loads.append(copy)

    barrier = pltpu.get_barrier_semaphore()
    for axis in range(3):
        for d in FAR_FIRST:
            for across in (0, 1):
                pl.semaphore_signal(barrier, inc=1, device_id=peer(axis, d, across), device_id_type=MESH)
    pl.semaphore_signal(barrier, inc=1, device_id=sibling, device_id_type=MESH)

    load_test.wait()

    my_rows = pl.ds(pl.multiple_of(64 * y, 64), 64)
    first_copies = []
    for i, block in enumerate(blocks):
        loads[2 * i].wait()
        loads[2 * i + 1].wait()
        product = jnp.dot(test_ref[...], a_ref[:, points(block)], preferred_element_type=f32).astype(bf16)
        if i == 0:
            pl.semaphore_wait(barrier, 19)
        if i < 3:
            yown[i] = product
            first_copies.append(
                send(peer(1, FAR_FIRST[i]), yown.at[i], basis.at[my_rows, :], y_ss.at[i], y_rs.at[i])
            )
        else:
            basis[my_rows, :] = product
    for copy in first_copies:
        copy.wait()

    half = pl.ds(pl.multiple_of(128 * core, 128), 128)
    other = pl.ds(pl.multiple_of(128 * (1 - core), 128), 128)
    g_own = pl.multiple_of(192 * core, 64)
    g_other = pl.multiple_of(192 * (1 - core), 64)

    def order(g):
        return g % 3, (g + 1) % 3, (g + 2) % 3

    def days(u):
        return slice(STARTS[u], STARTS[u + 1])

    def rows_of(i):
        return pl.ds(pl.multiple_of(32 * i, 32), 32)

    def one_pass(k, carry):
        last = k == PASSES - 1
        now, before = k % 2, (k + 1) % 2
        def send_three(axis, pair, ss, rs, three):
            for d in FAR_FIRST:
                src, dst = pair(d)
                send(peer(axis, d), src, dst, ss, rs)
            return copy_to(sibling, three, three, ss, rs)

        def full_block(d):
            block = points((y + d) % 4)
            product = jnp.dot(wf[before], a_ref[:, block], preferred_element_type=f32).astype(bf16)
            full[:, block] = (jnp.dot(inv_ref[...], product, preferred_element_type=f32) * (1.0 / POINTS)).astype(bf16)

        gram = lax.dot_general(basis[...], basis[...], (((1,), (1,)), ((), ())), preferred_element_type=f32)
        gp[:ROWS, :] = gram[:, :128].astype(bf16)
        gp[ROWS:, :] = gram[128:, 128:].astype(bf16)

        w_core = []

        def product_unit(u):
            wp[:, days(u)] = lax.dot_general(
                basis[...], a_ref[days(u), points(y)], (((1,), (1,)), ((), ())), preferred_element_type=f32
            ).astype(bf16)
            w_core.append(send(sibling, wp.at[other, days(u)], wc.at[:, days(u)], wc_ss.at[0], wc_rs.at[0, u]))

        def gram_send(stage, buf, g, value):
            axis = order(g)[stage]
            mine = buf.at[g, at[axis]]
            mine[...] = value.astype(bf16)
            return send_three(axis, lambda d: (mine, mine), g_ss.at[stage], g_rs.at[stage, g], buf.at[g, 0:3])

        def gram_sum(arrived, buf, g):
            arrived.wait_recv()
            parts = [buf[g, i].astype(f32) for i in range(4)]
            return (parts[0] + parts[1]) + (parts[2] + parts[3])

        def four(buf, u):
            parts = [buf[u, i, :, : WIDTHS[u]].astype(f32) for i in range(4)]
            return ((parts[0] + parts[1]) + (parts[2] + parts[3])).astype(bf16)

        def slots(buf, u):
            return buf.at[u, 0:3, :, : WIDTHS[u]]

        ws1 = []

        def scatter(u):
            w_core[u].wait_recv()
            ws[:, days(u)] = (wp[half, days(u)].astype(f32) + wc[:, days(u)].astype(f32)).astype(bf16)
            axis = order(u)[0]
            ws1.append(
                send_three(
                    axis,
                    lambda d: (ws.at[rows_of((at[axis] + d) % 4), days(u)], r1.at[u, d - 1, :, : WIDTHS[u]]),
                    w_ss.at[0], w_rs.at[0, u], slots(r1, u),
                )
            )

        gs1 = []
        for g in range(3):
            slot = 4 * core + at[g]
            mine = gp.at[pl.ds(g_own + 64 * g, 64), :]
            theirs = gp.at[pl.ds(g_other + 64 * g, 64), :]
            for d in FAR_FIRST:
                send(peer(g, d, 1), theirs, g1.at[g, slot], g_ss.at[0], g_rs.at[0, g])
                send(peer(g, d), mine, g1.at[g, slot], g_ss.at[0], g_rs.at[0, g])
            send(sibling, theirs, g1.at[g, slot], g_ss.at[0], g_rs.at[0, g])
            g1[g, slot] = mine[...]
            gs1.append(copy_to(sibling, g1.at[g, 0:7], g1.at[g, 0:7], g_ss.at[0], g_rs.at[0, g]))

        for u in range(UNITS):
            product_unit(u)
            if u >= AHEAD:
                scatter(u - AHEAD)
        for u in range(UNITS - AHEAD, UNITS):
            scatter(u)

        pl.when(last)(lambda: full_block(1))

        gs2 = []
        for g in range(3):
            gs1[g].wait_recv()
            parts = [g1[g, i].astype(f32) for i in range(8)]
            total = ((parts[0] + parts[1]) + (parts[2] + parts[3])) + ((parts[4] + parts[5]) + (parts[6] + parts[7]))
            gs2.append(gram_send(1, g2, g, total))

        ws2 = []
        for u in range(UNITS):
            ws1[u].wait_recv()
            first, axis, _ = order(u)
            total = ws[rows_of(at[first]), days(u)].astype(f32)
            for d in range(3):
                total += r1[u, d, :, : WIDTHS[u]].astype(f32)
            mine = x2.at[u, at[axis], :, : WIDTHS[u]]
            mine[...] = total.astype(bf16)
            ws2.append(send_three(axis, lambda d, m=mine: (m, m), w_ss.at[1], w_rs.at[1, u], slots(x2, u)))

        pl.when(last)(lambda: full_block(2))

        gs3 = [gram_send(2, g3, g, gram_sum(gs2[g], g2, g)) for g in range(3)]

        ws3 = []
        for u in range(UNITS):
            ws2[u].wait_recv()
            axis = order(u)[2]
            mine = x3.at[u, at[axis], :, : WIDTHS[u]]
            mine[...] = four(x2, u)
            ws3.append(send_three(axis, lambda d, m=mine: (m, m), w_ss.at[2], w_rs.at[2, u], slots(x3, u)))

        @pl.when(last)
        def _():
            full_block(3)
            full[:, points(y)] = basis[...]

        ws4, pieces = [], []

        def finish(u):
            ws3[u].wait_recv()
            piece = wf.at[now, rows_of(4 * core + at[order(u)[0]]), days(u)]
            piece[...] = four(x3, u)
            pieces.append(piece)

        def send_back(u):
            ws4.append(
                send_three(
                    order(u)[0], lambda d: (pieces[u], pieces[u]), w_ss.at[3], w_rs.at[3, u], slots(x3, u)
                )
            )

        def gram_back():
            for g in range(3):
                gf[pl.ds(g_own + 64 * g, 64), :] = gram_sum(gs3[g], g3, g)
            mine = gf.at[pl.ds(g_own, 192), :]
            return send(sibling, mine, mine, gc_ss.at[1], gc_rs.at[1])

        def build():
            g_back.wait_recv()
            quarter = (128, 128)
            on = lax.broadcasted_iota(jnp.int32, quarter, 0) == lax.broadcasted_iota(jnp.int32, quarter, 1)
            upper, cross, lower = gf[:128, :], gf[128:ROWS, :], gf[ROWS:, :]
            diagonal = [jnp.where(on, upper, 0.0), jnp.where(on, lower, 0.0)]
            across = [lax.rsqrt(jnp.sum(v, axis=0, keepdims=True)) for v in diagonal]
            down = [lax.rsqrt(jnp.sum(v, axis=1, keepdims=True)) for v in diagonal]
            cross = cross * down[1] * across[0]
            t_ref[:128, :128] = upper * down[0] * across[0]
            t_ref[128:, 128:] = lower * down[1] * across[1]
            t_ref[128:, :128] = cross
            t_ref[:128, 128:] = cross.T
            norm_ref[...] = jnp.concatenate(across, axis=1) * POINTS**0.5

        def share(u):
            ws4[u].wait_recv()
            mine = wf.at[now, half, days(u)]
            return send(sibling, mine, mine, wc_ss.at[1], wc_rs.at[1, u])

        def use(batch):
            for u in range(BATCHES[batch], BATCHES[batch + 1]):
                w_back[u].wait_recv()
            own = slice(STARTS[BATCHES[batch]], STARTS[BATCHES[batch + 1]])
            product = jnp.dot(wf[now, :, own], a_ref[own, points(y)], preferred_element_type=f32)
            yacc[...] = product if batch == 0 else yacc[...] + product

        w_back = []
        step = 0
        for what, n in SCHEDULE:
            if what == "gram":
                g_back = gram_back()
            elif what == "back":
                for u in range(len(pieces), n):
                    finish(u)
                    send_back(u)
            elif what == "close":
                for u in range(UNITS - 3, UNITS):
                    finish(u)
                for u in range(UNITS - 3, UNITS):
                    send_back(u)
            elif what == "build":
                build()
            elif what == "factor":
                for _ in range(n):
                    factor_step(t_ref, step)
                    step += 1
            elif what == "share":
                for u in range(len(w_back), n):
                    w_back.append(share(u))
            else:
                use(n)

        stage = wp.at[0:96, :]
        for i in range(3):
            copy_to(sibling, stage, stage, w_ss.at[i], w_rs.at[i, 0]).wait_send()
        for i, three in enumerate((g1.at[:, 0:7], g2.at[:, 0:3], g2.at[:, 0:3])):
            copy_to(sibling, three, three, g_ss.at[i], g_rs.at[i, 0]).wait_send()
        copy_to(sibling, wc, wc, wc_ss.at[0], wc_rs.at[0, 0]).wait_send()

        inverse = (t_ref[...] * norm_ref[...]).astype(bf16)
        inv_ref[...] = inverse
        basis[...] = (
            jnp.dot(inverse, yacc[...].astype(bf16), preferred_element_type=f32) * (1.0 / POINTS)
        ).astype(bf16)

        copy_to(sibling, stage, stage, w_ss.at[3], w_rs.at[3, 0]).wait_send()
        copy_to(sibling, wc, wc, wc_ss.at[1], wc_rs.at[1, 0]).wait_send()
        g_back.wait_send()
        return carry

    lax.fori_loop(0, PASSES, one_pass, 0)

    own_inverse = inv_ref[my_rows, :]
    eofs_ref[...] = jnp.dot(own_inverse, full[...], preferred_element_type=f32)
    pcs_ref[...] = jnp.dot(own_inverse, wf[(PASSES - 1) % 2, :, :], preferred_element_type=f32) * (1.0 / POINTS)


def body(test_matrix, anomalies):
    vmem = pl.BlockSpec(memory_space=pltpu.VMEM)
    hbm = pl.BlockSpec(memory_space=pl.ANY)
    dma = pltpu.SemaphoreType.DMA
    return pl.pallas_call(
        kernel,
        out_shape=(jax.ShapeDtypeStruct((64, LOCAL), f32), jax.ShapeDtypeStruct((64, DAYS), f32)),
        in_specs=[hbm, hbm],
        out_specs=(vmem, vmem),
        scratch_shapes=[
            pltpu.VMEM((64, DAYS), bf16),
            pltpu.VMEM((DAYS, LOCAL), bf16),
            pltpu.VMEM((3, 64, OWN), bf16),
            pltpu.VMEM((ROWS, OWN), f32),
            pltpu.VMEM((ROWS, OWN), bf16),
            pltpu.VMEM((ROWS, LOCAL), bf16),
            pltpu.VMEM((ROWS, ROWS), bf16),
            pltpu.VMEM((ROWS, ROWS), f32),
            pltpu.VMEM((1, ROWS), f32),
            pltpu.VMEM((ROWS, DAYS), bf16),
            pltpu.VMEM((128, DAYS), bf16),
            pltpu.VMEM((128, DAYS), bf16),
            pltpu.VMEM((2, ROWS, DAYS), bf16),
            pltpu.VMEM((UNITS, 3, 32, WIDEST), bf16),
            pltpu.VMEM((UNITS, 4, 32, WIDEST), bf16),
            pltpu.VMEM((UNITS, 4, 32, WIDEST), bf16),
            pltpu.VMEM((384, 128), bf16),
            pltpu.VMEM((3, 8, 64, 128), bf16),
            pltpu.VMEM((3, 4, 64, 128), bf16),
            pltpu.VMEM((3, 4, 64, 128), bf16),
            pltpu.VMEM((384, 128), f32),
            dma((1,)),
            dma((4, 2)),
            dma((3,)),
            dma((3,)),
            dma((2,)),
            dma((2, UNITS)),
            dma((4,)),
            dma((4, UNITS)),
            dma((2,)),
            dma((2,)),
            dma((3,)),
            dma((3, 3)),
        ],
        compiler_params=pltpu.CompilerParams(collective_id=0, has_side_effects=True, vmem_limit_bytes=52 << 20),
        cost_estimate=pl.CostEstimate(flops=20 * 10**9, bytes_accessed=16 * 10**6, transcendentals=0),
        name="subspace_iteration",
    )(test_matrix, anomalies)


def solution(mesh):
    return jax.shard_map(
        body,
        mesh=mesh,
        in_specs=(P("col", None), P(None, "space")),
        out_specs=(P("col", "space"), P("col", None)),
        check_vma=False,
    )
```
